256 devices in a mesh: blk: 64 (over x, z_lo, y, core), pair: 4 (over z_hi).
Axes of the slice: x: 4, y: 4, z: 8 (z_hi: 4, z_lo: 2; z = z_hi * 2 + z_lo), core: 2. Of those that a mesh axis runs over, the one named last changes fastest.
Arguments:
- features: bfloat16 [4, 8192, 256], P('pair', 'blk'), may hold values from -4 to 4
- last_features: bfloat16 [8192, 256], P('blk'), may hold values from -4 to 4
- growth: float32 [4, 8192], P('pair', 'blk'), may hold values from 0.5 to 2
- cell_counts: int32 [5], replicated, may hold values from 4096 to 8192
Outputs:
- source_potential: float32 [4, 8192], P('pair', 'blk')
- target_potential: float32 [4, 8192], P('pair', 'blk')
- row_mass: float32 [4, 8192], P('pair', 'blk')
The draws below stay inside these ranges and needn't reach their ends.
Inputs may be any that keep to these rules, and one draw needn't show every extreme that they name: Time point t holds cell_counts[t] cells, in its first slots.
All inputs are finite; a program needn't handle non-finite values.
Results may differ from the reference program's by a relative error of at most 0.0003.
Values may be sent and summed in bfloat16 or wider, within the bound.
No kernel may reach another device: no remote copies, remote signals or barrier semaphores. Data moves between devices by JAX's collectives and lax.ppermute only.
A program may use at most 64 MiB of HBM per device.

```python
import math
import jax
import jax.numpy as jnp
from jax import lax

F = 256
ITERS = 2
PAIRS = 4
TIMES = 5
CELLS = 8192


def place_ends(values, rng, low, top_value):
    index_at = [jax.random.randint(jax.random.fold_in(rng, axis), (), 0, length) for axis, length in enumerate(values.shape)]
    widest = values.shape.index(max(values.shape))
    next_to = index_at[:widest] + [(index_at[widest] + 1) % values.shape[widest]] + index_at[widest + 1:]
    return values.at[tuple(index_at)].set(low).at[tuple(next_to)].set(top_value)


def shard_levels(rng, extent, shards, low, high):
    def one(axis_at, shards_of):
        draws = jax.random.uniform(jax.random.fold_in(jax.random.fold_in(rng, 6), axis_at), (shards_of,), jnp.float32, low / len(shards), high / len(shards))
        return jnp.repeat(jnp.exp(draws), extent[axis_at] // shards_of).reshape((-1,) + (1,) * (len(extent) - axis_at - 1))

    gain = one(*shards[0])
    for cut in shards[1:]:
        gain = gain * one(*cut)
    return gain


def centred(key, shape, deviation, limit, shards=(), held_as=jnp.bfloat16):
    array = deviation * jax.random.normal(key, shape, jnp.float32)
    if shards:
        array = array * shard_levels(key, shape, shards, -0.22, 0.18)
    return jnp.clip(array, -limit, limit).astype(held_as)


def setup_inputs(seed: int = 0) -> dict:
    splits = jax.random.split(jax.random.key(seed), 5)
    return {
        "features": centred(splits[0], (PAIRS, CELLS, F), 1.0, 4.0, ((0, 4), (1, 64))),
        "last_features": centred(splits[1], (CELLS, F), 1.0, 4.0, ((0, 64),)),
        "growth": jnp.clip(jnp.exp(math.log(2.0) - 1.3862944 * jax.random.uniform(splits[2], (PAIRS, CELLS), jnp.float32) ** shard_levels(splits[2], (PAIRS, CELLS), ((0, 4), (1, 64)), -0.2, 0.2)), 0.5, 2.0),
        "cell_counts": place_ends(jax.random.randint(splits[3], (TIMES,), CELLS // 2, CELLS + 1), jax.random.fold_in(splits[3], 1), CELLS // 2, CELLS).astype(jnp.int32),
    }


EPSILON = 0.1
PENALTY = 1.0


def cost_block(row_block, row_norms, columns, column_norms, inverse_scale):
    products = jnp.dot(row_block.astype(jnp.float32), columns.astype(jnp.float32).T, precision=lax.Precision.HIGHEST)
    return inverse_scale * (row_norms[:, None] + column_norms[None, :] - 2.0 * products)


def one_pair(source, target, growth_row, count_source, count_target):
    cell_total = source.shape[0]
    span_cols = math.gcd(cell_total, 512)
    number_blocks = cell_total // span_cols
    position = jnp.arange(cell_total, dtype=jnp.int32)
    source_present = position < count_source
    target_present = position < count_target
    source_widened = source.astype(jnp.float32)
    target_widened = target.astype(jnp.float32)
    source_norms = jnp.sum(source_widened * source_widened, axis=1)
    target_norms = jnp.sum(target_widened * target_widened, axis=1)
    source_count = count_source.astype(jnp.float32)
    target_count = count_target.astype(jnp.float32)
    source_mean = jnp.sum(jnp.where(source_present[:, None], source_widened, 0.0), axis=0) / source_count
    target_mean = jnp.sum(jnp.where(target_present[:, None], target_widened, 0.0), axis=0) / target_count
    spread = (jnp.sum(jnp.where(source_present, source_norms, 0.0)) / source_count
              + jnp.sum(jnp.where(target_present, target_norms, 0.0)) / target_count
              - 2.0 * jnp.sum(source_mean * target_mean))
    inverse_scale = 1.0 / (EPSILON * spread)
    exponent = PENALTY / (PENALTY + EPSILON)
    log_source = jnp.log(growth_row / source_count)
    log_target = -jnp.log(target_count)

    def row_sums(target_pot):
        def single(number):
            anchor = number * span_cols
            row_block = lax.dynamic_slice_in_dim(source, anchor, span_cols, 0)
            norms_here = lax.dynamic_slice_in_dim(source_norms, anchor, span_cols, 0)
            scores = cost_block(row_block, norms_here, target, target_norms, inverse_scale)
            summands = jnp.where(target_present[None, :], jnp.exp(target_pot[None, :] - scores), 0.0)
            return jnp.sum(summands, axis=1)
        return lax.map(single, jnp.arange(number_blocks, dtype=jnp.int32)).reshape(cell_total)

    def column_sums(source_pot):
        def advance(running, number):
            anchor = number * span_cols
            row_block = lax.dynamic_slice_in_dim(source, anchor, span_cols, 0)
            norms_here = lax.dynamic_slice_in_dim(source_norms, anchor, span_cols, 0)
            pots_here = lax.dynamic_slice_in_dim(source_pot, anchor, span_cols, 0)
            present_here = lax.dynamic_slice_in_dim(source_present, anchor, span_cols, 0)
            scores = cost_block(row_block, norms_here, target, target_norms, inverse_scale)
            summands = jnp.where(present_here[:, None], jnp.exp(pots_here[:, None] - scores), 0.0)
            return running + jnp.sum(summands, axis=0), None
        running, _ = lax.scan(advance, jnp.zeros((cell_total,), jnp.float32), jnp.arange(number_blocks, dtype=jnp.int32))
        return running

    target_pot = jnp.zeros((cell_total,), jnp.float32)
    source_pot = jnp.zeros((cell_total,), jnp.float32)
    for repeat in range(ITERS):
        sums_rows = row_sums(target_pot)
        source_pot = jnp.where(source_present, exponent * (log_source - jnp.log(sums_rows)), 0.0)
        sums_cols = column_sums(source_pot)
        target_pot = jnp.where(target_present, exponent * (log_target - jnp.log(sums_cols)), 0.0)
    sums_rows = row_sums(target_pot)
    row_mass = jnp.where(source_present, source_count * jnp.exp(source_pot) * sums_rows, 0.0)
    return source_pot, target_pot, row_mass


def reference(features, last_features, growth, cell_counts):
    sources_out = []
    targets_out = []
    masses_out = []
    for moment in range(PAIRS):
        target = features[moment + 1] if moment + 1 < PAIRS else last_features
        source_pot, target_pot, row_mass = one_pair(features[moment], target, growth[moment], cell_counts[moment], cell_counts[moment + 1])
        sources_out.append(source_pot)
        targets_out.append(target_pot)
        masses_out.append(row_mass)
    return (jnp.stack(sources_out), jnp.stack(targets_out), jnp.stack(masses_out))
```

```python
import functools
import math

import jax
import jax.numpy as jnp
from jax import lax
from jax.experimental import pallas as pl
from jax.experimental.pallas import tpu as pltpu
from jax.sharding import Mesh
from jax.sharding import PartitionSpec as P

AXES = ("x", "z", "y", "c", "g")
SIZES = (4, 2, 4, 2, 4)
ROW_AXES = ("z", "c")
COLUMN_AXES = ("x", "y")
BACK_AXES = ("z", "c", "g")

EPSILON = 0.1
PENALTY = 1.0
TAU = PENALTY / (PENALTY + EPSILON)
LOG2E = math.log2(math.e)
ABSENT = -1e30

CELLS = 128
ROW_BLOCKS = 4
COLUMN_BLOCKS = 16
ROWS = ROW_BLOCKS * CELLS
COLUMNS = COLUMN_BLOCKS * CELLS
STRIP = 64

F32 = jnp.float32


def shape(*dims, dtype=F32):
    return jax.ShapeDtypeStruct(dims, dtype)


def call(kernel, out_shape, n_inputs, scratch=(), flops=0, name=None):
    vmem = pl.BlockSpec(memory_space=pltpu.VMEM)
    return pl.pallas_call(
        kernel,
        out_shape=out_shape,
        in_specs=[pl.BlockSpec(memory_space=pltpu.SMEM)] + [vmem] * n_inputs,
        out_specs=jax.tree.map(lambda _: vmem, out_shape),
        scratch_shapes=list(scratch),
        compiler_params=pltpu.CompilerParams(vmem_limit_bytes=20 * 1024 * 1024),
        name=name,
    )


def lanes():
    return lax.broadcasted_iota(jnp.int32, (1, CELLS), 1)


def block_start(x, z, y, c):
    return (((x * 2 + z) * 4 + y) * 2 + c) * CELLS


def counts_of(counts):
    t = lax.rem(lax.axis_index("g") + 3, 4)
    return counts[t], counts[t + 1]


def row_positions(k):
    place = (lax.axis_index("z") * 2 + lax.axis_index("c")) ^ k
    return block_start(lax.axis_index("x"), place >> 1, lax.axis_index("y"), place & 1) + lanes()


def column_positions():
    block = lax.broadcasted_iota(jnp.int32, (COLUMN_BLOCKS, CELLS), 0)
    lane = lax.broadcasted_iota(jnp.int32, (COLUMN_BLOCKS, CELLS), 1)
    return block_start(block >> 2, lax.axis_index("z"), block & 3, lax.axis_index("c")) + lane


def own_start():
    return block_start(*(lax.axis_index(a) for a in ("x", "z", "y", "c")))


def local_sums(counts, features, last, growth, x_message, y_message):
    g = lax.axis_index("g")
    row = own_start() + lax.broadcasted_iota(jnp.int32, (CELLS, 1), 0)
    wide = features[0].astype(F32)
    targets = jnp.where(g == 0, last[...].astype(F32), wide)
    _, count_target = counts_of(counts)
    for cells, count, message in ((wide, counts[g], x_message), (targets, count_target, y_message)):
        present = row < count
        squares = cells * cells
        halves = squares[:, :CELLS] + squares[:, CELLS:]
        kept = jnp.where(present, cells, 0.0)
        total = jnp.sum(kept, axis=0, keepdims=True)
        message[0:1, :] = total[:, :CELLS]
        message[1:2, :] = total[:, CELLS:]
        norms = jnp.sum(halves.T, axis=0, keepdims=True)
        here = own_start() + lanes() < count
        norm_total = jnp.sum(jnp.where(here, norms, 0.0), axis=1, keepdims=True)
        message[2:3, :] = jnp.broadcast_to(norm_total, (1, CELLS))
        message[3:4, :] = growth[...] if message is x_message else norms
        message[4:8, :] = jnp.zeros((4, CELLS), F32)


def merged_sums(counts, x0, x1, x2, x3, y0, y1, y2, y3, out):
    x = x0[...] + x1[...] + x2[...] + x3[...]
    y = y0[...] + y1[...] + y2[...] + y3[...]
    row = lax.broadcasted_iota(jnp.int32, (8, CELLS), 0)
    shifted = jnp.concatenate([y[4:8], y[0:4]], axis=0)
    both = jnp.where(row < 4, x, shifted)
    both = jnp.where(row == 7, y0[3:4, :], both)
    out[...] = jnp.broadcast_to(both[None], out.shape)


def lane_sums(part, k):
    return jnp.sum(part[k * CELLS : (k + 1) * CELLS, :].T, axis=0, keepdims=True)


def first_pass(counts, moments, x0, x1, x2, x3, targets, scores, sums, rows, weights, part, limits):
    count_source, count_target = counts_of(counts)
    total = jnp.sum(moments[...], axis=0)
    n_s = count_source.astype(F32)
    n_t = count_target.astype(F32)
    products = (total[0:2] / n_s) * (total[4:6] / n_t)
    dot = jnp.sum(jnp.sum(products, axis=0, keepdims=True), axis=1, keepdims=True)
    spread = total[2:3, 0:1] / n_s + total[6:7, 0:1] / n_t - 2.0 * dot
    scale = LOG2E / (EPSILON * spread)
    for k, block in enumerate((x0, x1, x2, x3)):
        rows[k * CELLS : (k + 1) * CELLS, :] = block[0]
        wide = block[0].astype(F32)
        norms = jnp.sum(wide * wide, axis=1, keepdims=True)
        weights[k * CELLS : (k + 1) * CELLS, :] = jnp.broadcast_to(norms * scale, (CELLS, CELLS))
    part[...] = jnp.zeros_like(part)
    limits[...] = jnp.where(column_positions() < count_target, 0.0, ABSENT)
    twice = 2.0 * scale

    @pl.loop(0, COLUMN_BLOCKS // 2)
    def _(pair):
        first = pair * 2
        block = targets[pl.ds(first, 2)].reshape(2 * CELLS, 256)
        products = lax.dot_general(
            rows[...], block, (((1,), (1,)), ((), ())), preferred_element_type=F32
        )
        running = part[...]
        for half in range(2):
            norms = moments[first + half, 7:8, :] * scale
            limit = limits[pl.ds(first + half, 1), :]
            tile = (weights[...] + norms) - twice * products[:, half * CELLS : (half + 1) * CELLS]
            scores[first + half] = tile
            running = running + jnp.exp2(limit - tile)
        part[...] = running

    for k in range(ROW_BLOCKS):
        sums[k : k + 1, :] = lane_sums(part, k)


def column_pass(counts, own, p1, p2, p3, m0, m1, m2, m3, scores, alphas, out, spread_out, gathered):
    count_source, _ = counts_of(counts)
    n_s = count_source.astype(F32)
    for k, message in enumerate((m0, m1, m2, m3)):
        total = own[k : k + 1, :]
        for j, other in ((1, p1), (2, p2), (3, p3)):
            total = total + other[(k ^ j) : (k ^ j) + 1, :]
        alpha = TAU * (jnp.log(message[3:4, :] / n_s) - jnp.log(total))
        present = row_positions(k) < count_source
        alphas[k : k + 1, :] = jnp.where(present, alpha, 0.0)
        limit = jnp.where(present, alpha * LOG2E, ABSENT)
        spread_out[k * CELLS : (k + 1) * CELLS, :] = jnp.broadcast_to(limit, (CELLS, CELLS)).T

    @pl.loop(0, COLUMN_BLOCKS)
    def _(block):
        def strip(number, running):
            at = pl.ds(number * STRIP, STRIP)
            terms = jnp.exp2(spread_out[at, :] - scores[block, at, :])
            return running + jnp.sum(terms.reshape(STRIP // 8, 8, CELLS), axis=0)

        total = lax.fori_loop(0, ROWS // STRIP, strip, jnp.zeros((8, CELLS), F32), unroll=True)
        gathered[pl.ds(block, 1), :] = jnp.sum(total, axis=0, keepdims=True)

    out[...] = jnp.broadcast_to(gathered[...][None], out.shape)


def row_sums(counts, parts, scores, part, limits):
    _, count_target = counts_of(counts)
    n_t = jnp.full((1, CELLS), 1, F32) * count_target.astype(F32)
    total = jnp.sum(parts[...], axis=0)
    beta = TAU * (-jnp.log(n_t) - jnp.log(total))
    present = column_positions() < count_target
    limits[...] = jnp.where(present, beta * LOG2E, ABSENT)
    part[...] = jnp.zeros_like(part)

    @pl.loop(0, COLUMN_BLOCKS // 2)
    def _(pair):
        first = pair * 2
        terms = jnp.exp2(limits[pl.ds(first, 1), :] - scores[first])
        more = jnp.exp2(limits[pl.ds(first + 1, 1), :] - scores[first + 1])
        part[...] += terms + more

    return jnp.where(present, beta, 0.0)


def row_pass(counts, parts, scores, sums, part, limits):
    row_sums(counts, parts, scores, part, limits)
    for k in range(ROW_BLOCKS):
        sums[k : k + 1, :] = lane_sums(part, k)


def last_row_pass(counts, parts, scores, alphas, beta_out, q0, q1, q2, q3, part, limits, betas):
    betas[...] = row_sums(counts, parts, scores, part, limits)
    place = lax.axis_index("x") * 4 + lax.axis_index("y")
    beta_out[...] = betas[pl.ds(place, 1), :]
    count_source, _ = counts_of(counts)
    n_s = count_source.astype(F32)
    for k, out in enumerate((q0, q1, q2, q3)):
        mass = n_s * jnp.exp(alphas[k : k + 1, :]) * lane_sums(part, k)
        out[...] = jnp.where(row_positions(k) < count_source, mass, 0.0)


def forward(value, k):
    moves = [(d * 4 + g, (d ^ k) * 4 + (g + 1) % 4) for d in range(4) for g in range(4)]
    return lax.ppermute(value, BACK_AXES, moves)


def backward(value, k):
    moves = [(d * 4 + g, (d ^ k) * 4 + (g - 1) % 4) for d in range(4) for g in range(4)]
    return lax.ppermute(value, BACK_AXES, moves)


def across(value, k):
    return lax.ppermute(value, ROW_AXES, [(d, d ^ k) for d in range(4)])


def exchanged(copies):
    return lax.all_to_all(copies, COLUMN_AXES, split_axis=0, concat_axis=0, tiled=True)


def local(features, last_features, growth, cell_counts):
    part = pltpu.VMEM((ROWS, CELLS), F32)
    limits = pltpu.VMEM((COLUMN_BLOCKS, CELLS), F32)
    every_score = shape(COLUMN_BLOCKS, ROWS, CELLS)

    with jax.named_scope("gather"):
        targets = jnp.where(lax.axis_index("g") == 0, last_features, features[0])
        targets = exchanged(jnp.broadcast_to(targets[None], (COLUMN_BLOCKS, CELLS, 256)))
        sources = [forward(features, k) for k in range(ROW_BLOCKS)]

    with jax.named_scope("moments"):
        x_message, y_message = call(
            local_sums, (shape(8, CELLS), shape(8, CELLS)), 3, name="local_sums"
        )(cell_counts, features, last_features, growth)
        x_messages = [forward(x_message, k) for k in range(ROW_BLOCKS)]
        y_messages = [y_message] + [across(y_message, k) for k in range(1, ROW_BLOCKS)]
        moments = exchanged(
            call(merged_sums, shape(COLUMN_BLOCKS, 8, CELLS), 8, name="merged_sums")(
                cell_counts, *x_messages, *y_messages
            )
        )

    def row_exchange(sums):
        return [sums] + [across(sums, k) for k in range(1, ROW_BLOCKS)]

    columns = call(
        column_pass,
        (shape(ROW_BLOCKS, CELLS), shape(COLUMN_BLOCKS, COLUMN_BLOCKS, CELLS)),
        9,
        (part, limits),
        name="column_pass",
    )
    with jax.named_scope("first_rows"):
        scores, sums = call(
            first_pass,
            (every_score, shape(ROW_BLOCKS, CELLS)),
            6,
            (pltpu.VMEM((ROWS, 256), jnp.bfloat16), part, part, limits),
            name="first_pass",
        )(cell_counts, moments, *sources, targets)
    with jax.named_scope("first_columns"):
        _, copies = columns(cell_counts, *row_exchange(sums), *x_messages, scores)
        parts = exchanged(copies)
    with jax.named_scope("second_rows"):
        sums = call(
            row_pass, shape(ROW_BLOCKS, CELLS), 2, (part, limits), name="row_pass"
        )(cell_counts, parts, scores)
    with jax.named_scope("second_columns"):
        alphas, copies = columns(cell_counts, *row_exchange(sums), *x_messages, scores)
        source_pot = backward(alphas[0:1], 0)
        parts = exchanged(copies)
    with jax.named_scope("mass"):
        target_pot, *masses = call(
            last_row_pass,
            (shape(1, CELLS),) * 5,
            3,
            (part, limits, limits),
            name="last_row_pass",
        )(cell_counts, parts, scores, alphas)
        target_pot = backward(target_pot, 0)
        masses = [backward(mass, k) for k, mass in enumerate(masses)]
        row_mass = (masses[0] + masses[1]) + (masses[2] + masses[3])
    return source_pot, target_pot, row_mass


def solution(mesh):
    fine = Mesh(mesh.devices.reshape(SIZES), AXES)
    blk = ("x", "z", "y", "c")
    return jax.shard_map(
        local,
        mesh=fine,
        in_specs=(P("g", blk, None), P(blk, None), P("g", blk), P()),
        out_specs=(P("g", blk),) * 3,
        check_vma=False,
    )
```

```python
import math

import jax
import jax.numpy as jnp
from jax import lax
from jax.experimental import pallas as pl
from jax.experimental.pallas import tpu as pltpu
from jax.sharding import Mesh
from jax.sharding import PartitionSpec as P

AXES = ("x", "z", "y", "c", "g")
SIZES = (4, 2, 4, 2, 4)
ROW_AXES = ("z", "c")
COLUMN_AXES = ("x", "y")

EPSILON = 0.1
PENALTY = 1.0
TAU = PENALTY / (PENALTY + EPSILON)
LOG2E = math.log2(math.e)
ABSENT = -1e30

CELLS = 128
WIDTH = 256
ROW_BLOCKS = 4
COLUMN_BLOCKS = 16
ROWS = ROW_BLOCKS * CELLS
EXTRA = 16
STRIP = 64

COLUMNS_AT = 0
ROWS_AT = 16
N_S = 20
N_T = 21
GROWTH = 22
LAST_GROUP = 23
FRAME = 24

F32 = jnp.float32
BF16 = jnp.bfloat16


def shape(*dims, dtype=F32):
    return jax.ShapeDtypeStruct(dims, dtype)


def call(kernel, out_shape, n_inputs, scratch=(), space=pltpu.VMEM, name=None):
    return pl.pallas_call(
        kernel,
        out_shape=out_shape,
        in_specs=[pl.BlockSpec(memory_space=space)] * n_inputs,
        out_specs=jax.tree.map(lambda _: pl.BlockSpec(memory_space=pltpu.VMEM), out_shape),
        scratch_shapes=list(scratch),
        compiler_params=pltpu.CompilerParams(vmem_limit_bytes=16 * 1024 * 1024),
        name=name,
    )


def block_start(x, z, y, c):
    return (((x * 2 + z) * 4 + y) * 2 + c) * CELLS


def across_sums(cells, present):
    kept = jnp.where(present, cells, 0.0)
    total = jnp.sum(kept, axis=0, keepdims=True)
    squares = jnp.sum(kept * kept, axis=0, keepdims=True)
    norm = jnp.sum(squares, axis=1, keepdims=True)
    return total[:, :CELLS], total[:, CELLS:], jnp.broadcast_to(norm, (1, CELLS))


def local_sums(
    features, last, growth, counts, message, own_out, last_out, frame, own, final, rates, numbers, sems
):
    copies = [
        pltpu.make_async_copy(source, target, sems.at[i])
        for i, (source, target) in enumerate(
            ((features, own), (last, final), (growth, rates), (counts, numbers))
        )
    ]
    for copy in copies:
        copy.start()
    x, z, y, c, g = (lax.axis_index(a) for a in AXES)
    start = block_start(x, z, y, c)
    for copy in reversed(copies):
        copy.wait()
    count_source = numbers[g]
    count_target = numbers[g + 1]
    row = start + lax.broadcasted_iota(jnp.int32, (CELLS, 1), 0)
    pieces = [
        *across_sums(own[0].astype(F32), row < count_source),
        jnp.zeros((1, CELLS), F32),
        *across_sums(final[...].astype(F32), row < numbers[4]),
        jnp.zeros((1, CELLS), F32),
    ]
    for i, piece in enumerate(pieces):
        message[i : i + 1, :] = piece
    own_out[...] = own[0]
    last_out[...] = final[...]
    block = lax.broadcasted_iota(jnp.int32, (COLUMN_BLOCKS, CELLS), 0)
    lane = lax.broadcasted_iota(jnp.int32, (COLUMN_BLOCKS, CELLS), 1)
    target = block_start(block >> 2, z, block & 3, c) + lane
    frame[COLUMNS_AT : COLUMNS_AT + COLUMN_BLOCKS, :] = jnp.where(target < count_target, 1.0, 0.0)
    for k in range(ROW_BLOCKS):
        place = (z * 2 + c) ^ k
        source = block_start(x, place >> 1, y, place & 1) + lane[:1]
        frame[ROWS_AT + k : ROWS_AT + k + 1, :] = jnp.where(source < count_source, 1.0, 0.0)
    ones = jnp.ones((1, CELLS), F32)
    frame[N_S : N_S + 1, :] = ones * count_source.astype(F32)
    frame[N_T : N_T + 1, :] = ones * count_target.astype(F32)
    frame[GROWTH : GROWTH + 1, :] = rates[...]
    frame[LAST_GROUP : LAST_GROUP + 1, :] = ones * (g == 3).astype(F32)


def core_sums(mine, other, out):
    out[...] = mine[...] + other[...]


def three_terms(value):
    high = value.astype(BF16).astype(F32)
    rest = value - high
    middle = rest.astype(BF16).astype(F32)
    return high, middle, rest - middle


def parcel(frame, mine, across, back, back_across, shifted, last, out):
    is_last = frame[LAST_GROUP : LAST_GROUP + 1, :] > 0.0
    here = mine[...] + across[...]
    there = back[...] + back_across[...]
    wide_last = jnp.concatenate([is_last, is_last], axis=1)
    targets = jnp.where(wide_last, last[...].astype(F32), shifted[0].astype(F32))
    squares = targets * targets
    norms = jnp.sum((squares[:, :CELLS] + squares[:, CELLS:]).T, axis=0, keepdims=True)
    target_sums = jnp.where(is_last, here[4:8], there[0:4])
    extra = jnp.concatenate(
        [
            jnp.concatenate([here[0:1], here[1:2]], axis=1),
            jnp.concatenate([target_sums[0:1], target_sums[1:2]], axis=1),
            jnp.concatenate([here[2:3], target_sums[2:3]], axis=1),
            jnp.concatenate([norms, norms], axis=1),
        ],
        axis=0,
    )
    rows = jnp.concatenate([*three_terms(extra), jnp.zeros((4, WIDTH), F32)], axis=0)
    whole = jnp.concatenate([targets.astype(BF16), rows.astype(BF16)], axis=0)
    for i in range(COLUMN_BLOCKS):
        out[i] = whole


def lane_sums(part, k):
    return jnp.sum(part[k * CELLS : (k + 1) * CELLS, :].T, axis=0, keepdims=True)


def first_pass(frame, targets, x0, x1, x2, x3, scores, sums, rows, weights, part, limits, norms):
    extra = targets[:, CELLS:, :].astype(F32)
    extra = extra[:, 0:4] + extra[:, 4:8] + extra[:, 8:12]
    total = jnp.sum(extra, axis=0)
    n_s = frame[N_S : N_S + 1, :]
    n_t = frame[N_T : N_T + 1, :]
    means = total[0:1] * total[1:2]
    dot = jnp.sum(means, axis=1, keepdims=True) / n_s / n_t
    spread = total[2:3, :CELLS] / n_s + total[2:3, CELLS:] / n_t - 2.0 * dot
    scale = LOG2E / (EPSILON * spread)
    for k, block in enumerate((x0[...], x1[0], x2[0], x3[0])):
        at = slice(k * CELLS, (k + 1) * CELLS)
        rows[at, :] = block
        wide = block.astype(F32)
        weights[at, :] = jnp.sum(wide * wide, axis=1, keepdims=True) * scale
    for i in range(COLUMN_BLOCKS):
        norms[i : i + 1, :] = extra[i, 3:4, :CELLS] * scale
    part[...] = jnp.zeros_like(part)
    limits[...] = jnp.where(frame[COLUMNS_AT : COLUMNS_AT + COLUMN_BLOCKS, :] > 0.0, 0.0, ABSENT)
    twice = 2.0 * scale

    @pl.loop(0, COLUMN_BLOCKS // 2)
    def _(pair):
        first = pair * 2
        block = targets[pl.ds(first, 2), :CELLS, :].reshape(2 * CELLS, WIDTH)
        products = lax.dot_general(
            rows[...], block, (((1,), (1,)), ((), ())), preferred_element_type=F32
        )
        running = part[...]
        for half in range(2):
            at = pl.ds(first + half, 1)
            tile = (weights[...] + norms[at, :]) - twice * products[
                :, half * CELLS : (half + 1) * CELLS
            ]
            scores[first + half] = tile
            running = running + jnp.exp2(limits[at, :] - tile)
        part[...] = running

    for k in range(ROW_BLOCKS):
        sums[k : k + 1, :] = lane_sums(part, k)
    sums[4:5, :] = frame[GROWTH : GROWTH + 1, :]
    sums[5:8, :] = jnp.zeros((3, CELLS), F32)


def column_pass(frame, alpha, scores, out, spread_out, gathered):
    for k in range(ROW_BLOCKS):
        present = frame[ROWS_AT + k : ROWS_AT + k + 1, :] > 0.0
        limit = jnp.where(present, alpha[k] * LOG2E, ABSENT)
        spread_out[k * CELLS : (k + 1) * CELLS, :] = jnp.broadcast_to(limit, (CELLS, CELLS)).T

    def strip(number, running):
        at = pl.ds(pl.multiple_of(number * STRIP, STRIP), STRIP)
        limit = spread_out[at, :]
        more = []
        for i, total in enumerate(running):
            terms = jnp.exp2(limit - scores[i, at, :])
            more.append(total + jnp.sum(terms.reshape(STRIP // 8, 8, CELLS), axis=0))
        return tuple(more)

    zeros = (jnp.zeros((8, CELLS), F32),) * COLUMN_BLOCKS
    for i, total in enumerate(lax.fori_loop(0, ROWS // STRIP, strip, zeros)):
        gathered[i : i + 1, :] = jnp.sum(total, axis=0, keepdims=True)
    out[...] = jnp.broadcast_to(gathered[...][None], out.shape)


def new_alphas(frame, parts, log_p):
    alphas = []
    for k in range(ROW_BLOCKS):
        total = parts[0][k : k + 1, :]
        for j in range(1, ROW_BLOCKS):
            total = total + parts[j][(k ^ j) : (k ^ j) + 1, :]
        present = frame[ROWS_AT + k : ROWS_AT + k + 1, :] > 0.0
        alphas.append(jnp.where(present, TAU * (log_p[k] - jnp.log(total)), 0.0))
    return alphas


def first_columns(frame, p0, p1, p2, p3, scores, log_out, out, spread_out, gathered):
    n_s = frame[N_S : N_S + 1, :]
    parts = (p0, p1, p2, p3)
    log_p = [jnp.log(part[4:5, :] / n_s) for part in parts]
    for k in range(ROW_BLOCKS):
        log_out[k : k + 1, :] = log_p[k]
    column_pass(frame, new_alphas(frame, parts, log_p), scores, out, spread_out, gathered)


def last_columns(
    frame, log_p, p0, p1, p2, p3, scores, weights, alpha_out, out, spread_out, gathered
):
    n_s = frame[N_S : N_S + 1, :]
    log_rows = [log_p[k : k + 1, :] for k in range(ROW_BLOCKS)]
    alphas = new_alphas(frame, (p0, p1, p2, p3), log_rows)
    alpha_out[...] = alphas[0]
    for k in range(ROW_BLOCKS):
        present = frame[ROWS_AT + k : ROWS_AT + k + 1, :]
        weights[k : k + 1, :] = present * n_s * jnp.exp(alphas[k])
    column_pass(frame, alphas, scores, out, spread_out, gathered)


def row_pass(frame, parts, scores, part, limits):
    n_t = frame[N_T : N_T + 1, :]
    total = jnp.sum(parts[...], axis=0)
    beta = TAU * (-jnp.log(n_t) - jnp.log(total))
    present = frame[COLUMNS_AT : COLUMNS_AT + COLUMN_BLOCKS, :] > 0.0
    limits[...] = jnp.where(present, beta * LOG2E, ABSENT)

    @pl.loop(0, ROWS // STRIP)
    def _(number):
        at = pl.ds(pl.multiple_of(number * STRIP, STRIP), STRIP)
        running = jnp.exp2(limits[0:1, :] - scores[0, at, :])
        for i in range(1, COLUMN_BLOCKS):
            running = running + jnp.exp2(limits[i : i + 1, :] - scores[i, at, :])
        part[at, :] = running

    return jnp.where(present, beta, 0.0)


def second_rows(frame, parts, scores, sums, part, limits):
    row_pass(frame, parts, scores, part, limits)
    for k in range(ROW_BLOCKS):
        sums[k : k + 1, :] = lane_sums(part, k)


def last_rows(frame, parts, scores, weights, beta_out, q0, q1, q2, q3, part, limits, betas):
    betas[...] = row_pass(frame, parts, scores, part, limits)
    place = lax.axis_index("x") * 4 + lax.axis_index("y")
    beta_out[...] = betas[pl.ds(place, 1), :]
    for k, out in enumerate((q0, q1, q2, q3)):
        present = frame[ROWS_AT + k : ROWS_AT + k + 1, :] > 0.0
        out[...] = jnp.where(present, weights[k : k + 1, :] * lane_sums(part, k), 0.0)


def across(value, k):
    return lax.ppermute(value, ROW_AXES, [(d, d ^ k) for d in range(4)])


def back(value, k):
    moves = [(z * 4 + g, (z ^ k) * 4 + (g - 1) % 4) for z in range(2) for g in range(4)]
    return lax.ppermute(value, ("z", "g"), moves)


def exchanged(copies):
    return lax.all_to_all(copies, COLUMN_AXES, split_axis=0, concat_axis=0, tiled=True)


def local(features, last_features, growth, cell_counts):
    part = pltpu.VMEM((ROWS, CELLS), F32)
    limits = pltpu.VMEM((COLUMN_BLOCKS, CELLS), F32)
    some_cells = shape(CELLS, WIDTH, dtype=BF16)
    row_parts = shape(8, CELLS)
    column_parts = shape(COLUMN_BLOCKS, COLUMN_BLOCKS, CELLS)

    with jax.named_scope("moments"):
        shifted = back(features, 0)
        message, own, last, frame = call(
            local_sums,
            (row_parts, some_cells, some_cells, shape(FRAME, CELLS)),
            4,
            (
                pltpu.VMEM((1, CELLS, WIDTH), BF16),
                pltpu.VMEM((CELLS, WIDTH), BF16),
                pltpu.VMEM((1, CELLS), F32),
                pltpu.SMEM((5,), jnp.int32),
                pltpu.SemaphoreType.DMA((4,)),
            ),
            space=pltpu.HBM,
            name="local_sums",
        )(features, last_features, growth, cell_counts)
        other = lax.ppermute(message, "c", [(0, 1), (1, 0)])
        mine = call(core_sums, row_parts, 2, name="core_sums")(message, other)
        beside = lax.ppermute(mine, "z", [(0, 1), (1, 0)])
    with jax.named_scope("gather"):
        copies = call(
            parcel, shape(COLUMN_BLOCKS, CELLS + EXTRA, WIDTH, dtype=BF16), 7, name="parcel"
        )(frame, mine, beside, back(mine, 0), back(mine, 1), shifted, last)
        targets = exchanged(copies)
        sources = [own] + [across(features, k) for k in range(1, ROW_BLOCKS)]

    def row_exchange(sums):
        return [sums] + [across(sums, k) for k in range(1, ROW_BLOCKS)]

    with jax.named_scope("first_rows"):
        scores, sums = call(
            first_pass,
            (shape(COLUMN_BLOCKS, ROWS, CELLS), row_parts),
            6,
            (pltpu.VMEM((ROWS, WIDTH), BF16), part, part, limits, limits),
            name="first_pass",
        )(frame, targets, *sources)
    with jax.named_scope("first_columns"):
        log_p, copies = call(
            first_columns,
            (shape(ROW_BLOCKS, CELLS), column_parts),
            6,
            (part, limits),
            name="first_columns",
        )(frame, *row_exchange(sums), scores)
        parts = exchanged(copies)
    with jax.named_scope("second_rows"):
        sums = call(second_rows, shape(ROW_BLOCKS, CELLS), 3, (part, limits), name="second_rows")(
            frame, parts, scores
        )
    with jax.named_scope("last_columns"):
        weights, source_pot, copies = call(
            last_columns,
            (shape(ROW_BLOCKS, CELLS), shape(1, CELLS), column_parts),
            7,
            (part, limits),
            name="last_columns",
        )(frame, log_p, *row_exchange(sums), scores)
        parts = exchanged(copies)
    with jax.named_scope("mass"):
        target_pot, *masses = call(
            last_rows, (shape(1, CELLS),) * 5, 4, (part, limits, limits), name="last_rows"
        )(frame, parts, scores, weights)
        masses = [masses[0]] + [across(masses[k], k) for k in range(1, ROW_BLOCKS)]
        row_mass = (masses[0] + masses[1]) + (masses[2] + masses[3])
    return source_pot, target_pot, row_mass


def solution(mesh):
    fine = Mesh(mesh.devices.reshape(SIZES), AXES)
    blk = ("x", "z", "y", "c")
    return jax.shard_map(
        local,
        mesh=fine,
        in_specs=(P("g", blk, None), P(blk, None), P("g", blk), P()),
        out_specs=(P("g", blk),) * 3,
        check_vma=False,
    )
```

```python
import math

import jax
import jax.numpy as jnp
from jax import lax
from jax.experimental import pallas as pl
from jax.experimental.pallas import tpu as pltpu
from jax.sharding import Mesh
from jax.sharding import PartitionSpec as P

AXES = ("x", "z", "y", "c", "g")
SIZES = (4, 2, 4, 2, 4)
ROW_AXES = ("z", "c")
COLUMN_AXES = ("x", "y")

EPSILON = 0.1
PENALTY = 1.0
TAU = PENALTY / (PENALTY + EPSILON)
LOG2E = math.log2(math.e)
ABSENT = -1e30

CELLS = 128
WIDTH = 256
ROW_BLOCKS = 4
COLUMN_BLOCKS = 16
ROWS = ROW_BLOCKS * CELLS
EXTRA = 16
STRIP = 64

COLUMNS_AT = 0
ROWS_AT = 16
N_S = 20
N_T = 21
GROWTH = 22
LAST_GROUP = 23
FRAME = 24

F32 = jnp.float32
BF16 = jnp.bfloat16


def shape(*dims, dtype=F32):
    return jax.ShapeDtypeStruct(dims, dtype)


def call(kernel, out_shape, n_inputs, scratch=(), space=pltpu.VMEM, awaited=0, name=None):
    return pl.pallas_call(
        kernel,
        out_shape=out_shape,
        in_specs=[pl.BlockSpec(memory_space=space)] * n_inputs
        + [pl.BlockSpec(memory_space=pl.ANY)] * awaited,
        out_specs=jax.tree.map(lambda _: pl.BlockSpec(memory_space=pltpu.VMEM), out_shape),
        scratch_shapes=list(scratch),
        compiler_params=pltpu.CompilerParams(vmem_limit_bytes=16 * 1024 * 1024),
        name=name,
    )


def block_start(x, z, y, c):
    return (((x * 2 + z) * 4 + y) * 2 + c) * CELLS


def across_sums(cells, present):
    kept = jnp.where(present, cells, 0.0)
    total = jnp.sum(kept, axis=0, keepdims=True)
    squares = jnp.sum(kept * kept, axis=0, keepdims=True)
    norm = jnp.sum(squares, axis=1, keepdims=True)
    return total[:, :CELLS], total[:, CELLS:], jnp.broadcast_to(norm, (1, CELLS))


def local_sums(
    features, last, growth, counts, message, own_out, last_out, frame, own, final, rates, numbers, sems
):
    copies = [
        pltpu.make_async_copy(source, target, sems.at[i])
        for i, (source, target) in enumerate(
            ((features, own), (last, final), (growth, rates), (counts, numbers))
        )
    ]
    for copy in copies:
        copy.start()
    x, z, y, c, g = (lax.axis_index(a) for a in AXES)
    start = block_start(x, z, y, c)
    for copy in reversed(copies):
        copy.wait()
    count_source = numbers[g]
    count_target = numbers[g + 1]
    row = start + lax.broadcasted_iota(jnp.int32, (CELLS, 1), 0)
    pieces = [
        *across_sums(own[0].astype(F32), row < count_source),
        jnp.zeros((1, CELLS), F32),
        *across_sums(final[...].astype(F32), row < numbers[4]),
        jnp.zeros((1, CELLS), F32),
    ]
    for i, piece in enumerate(pieces):
        message[i : i + 1, :] = piece
    own_out[...] = own[0]
    last_out[...] = final[...]
    block = lax.broadcasted_iota(jnp.int32, (COLUMN_BLOCKS, CELLS), 0)
    lane = lax.broadcasted_iota(jnp.int32, (COLUMN_BLOCKS, CELLS), 1)
    target = block_start(block >> 2, z, block & 3, c) + lane
    frame[COLUMNS_AT : COLUMNS_AT + COLUMN_BLOCKS, :] = jnp.where(target < count_target, 1.0, 0.0)
    for k in range(ROW_BLOCKS):
        place = (z * 2 + c) ^ k
        source = block_start(x, place >> 1, y, place & 1) + lane[:1]
        frame[ROWS_AT + k : ROWS_AT + k + 1, :] = jnp.where(source < count_source, 1.0, 0.0)
    ones = jnp.ones((1, CELLS), F32)
    frame[N_S : N_S + 1, :] = ones * count_source.astype(F32)
    frame[N_T : N_T + 1, :] = ones * count_target.astype(F32)
    frame[GROWTH : GROWTH + 1, :] = rates[...]
    frame[LAST_GROUP : LAST_GROUP + 1, :] = ones * (g == 3).astype(F32)


def core_sums(mine, other, cells, other_cells, out, both):
    out[...] = mine[...] + other[...]
    both[:CELLS, :] = cells[...]
    both[CELLS:, :] = other_cells[...]


def three_terms(value):
    high = value.astype(BF16).astype(F32)
    rest = value - high
    middle = rest.astype(BF16).astype(F32)
    return high, middle, rest - middle


def parcel(frame, mine, across, back, back_across, shifted, last, sources, out):
    is_last = frame[LAST_GROUP : LAST_GROUP + 1, :] > 0.0
    here = mine[...] + across[...]
    there = back[...] + back_across[...]
    wide_last = jnp.concatenate([is_last, is_last], axis=1)
    targets = jnp.where(wide_last, last[...].astype(F32), shifted[...].astype(F32))
    squares = targets * targets
    norms = jnp.sum((squares[:, :CELLS] + squares[:, CELLS:]).T, axis=0, keepdims=True)
    target_sums = jnp.where(is_last, here[4:8], there[0:4])
    extra = jnp.concatenate(
        [
            jnp.concatenate([here[0:1], here[1:2]], axis=1),
            jnp.concatenate([target_sums[0:1], target_sums[1:2]], axis=1),
            jnp.concatenate([here[2:3], target_sums[2:3]], axis=1),
            jnp.concatenate([norms, norms], axis=1),
        ],
        axis=0,
    )
    rows = jnp.concatenate([*three_terms(extra), jnp.zeros((4, WIDTH), F32)], axis=0)
    whole = jnp.concatenate([targets.astype(BF16), rows.astype(BF16)], axis=0)
    for i in range(COLUMN_BLOCKS):
        out[i] = whole


def lane_sums(part, k):
    return jnp.sum(part[k * CELLS : (k + 1) * CELLS, :].T, axis=0, keepdims=True)


def first_pass(frame, targets, near, far, scores, sums, rows, weights, part, limits, norms):
    extra = targets[:, CELLS:, :].astype(F32)
    extra = extra[:, 0:4] + extra[:, 4:8] + extra[:, 8:12]
    total = jnp.sum(extra, axis=0)
    n_s = frame[N_S : N_S + 1, :]
    n_t = frame[N_T : N_T + 1, :]
    means = total[0:1] * total[1:2]
    dot = jnp.sum(means, axis=1, keepdims=True) / n_s / n_t
    spread = total[2:3, :CELLS] / n_s + total[2:3, CELLS:] / n_t - 2.0 * dot
    scale = LOG2E / (EPSILON * spread)
    for k, block in enumerate((near[...], far[...])):
        at = slice(k * 2 * CELLS, (k + 1) * 2 * CELLS)
        rows[at, :] = block
        wide = block.astype(F32)
        weights[at, :] = jnp.sum(wide * wide, axis=1, keepdims=True) * scale
    for i in range(COLUMN_BLOCKS):
        norms[i : i + 1, :] = extra[i, 3:4, :CELLS] * scale
    part[...] = jnp.zeros_like(part)
    limits[...] = jnp.where(frame[COLUMNS_AT : COLUMNS_AT + COLUMN_BLOCKS, :] > 0.0, 0.0, ABSENT)
    twice = 2.0 * scale

    @pl.loop(0, COLUMN_BLOCKS // 2)
    def _(pair):
        first = pair * 2
        block = targets[pl.ds(first, 2), :CELLS, :].reshape(2 * CELLS, WIDTH)
        products = lax.dot_general(
            rows[...], block, (((1,), (1,)), ((), ())), preferred_element_type=F32
        )
        running = part[...]
        for half in range(2):
            at = pl.ds(first + half, 1)
            tile = (weights[...] + norms[at, :]) - twice * products[
                :, half * CELLS : (half + 1) * CELLS
            ]
            scores[first + half] = tile
            running = running + jnp.exp2(limits[at, :] - tile)
        part[...] = running

    for k in range(ROW_BLOCKS):
        sums[k : k + 1, :] = lane_sums(part, k)
    sums[4:5, :] = frame[GROWTH : GROWTH + 1, :]
    sums[5:8, :] = jnp.zeros((3, CELLS), F32)


def column_pass(frame, alpha, scores, out, spread_out, gathered):
    for k in range(ROW_BLOCKS):
        present = frame[ROWS_AT + k : ROWS_AT + k + 1, :] > 0.0
        limit = jnp.where(present, alpha[k] * LOG2E, ABSENT)
        spread_out[k * CELLS : (k + 1) * CELLS, :] = jnp.broadcast_to(limit, (CELLS, CELLS)).T

    def strip(number, running):
        at = pl.ds(pl.multiple_of(number * STRIP, STRIP), STRIP)
        limit = spread_out[at, :]
        more = []
        for i, total in enumerate(running):
            terms = jnp.exp2(limit - scores[i, at, :])
            more.append(total + jnp.sum(terms.reshape(STRIP // 8, 8, CELLS), axis=0))
        return tuple(more)

    zeros = (jnp.zeros((8, CELLS), F32),) * COLUMN_BLOCKS
    for i, total in enumerate(lax.fori_loop(0, ROWS // STRIP, strip, zeros)):
        gathered[i : i + 1, :] = jnp.sum(total, axis=0, keepdims=True)
    out[...] = jnp.broadcast_to(gathered[...][None], out.shape)


def new_alphas(frame, parts, log_p):
    alphas = []
    for k in range(ROW_BLOCKS):
        total = parts[0][k : k + 1, :]
        for j in range(1, ROW_BLOCKS):
            total = total + parts[j][(k ^ j) : (k ^ j) + 1, :]
        present = frame[ROWS_AT + k : ROWS_AT + k + 1, :] > 0.0
        alphas.append(jnp.where(present, TAU * (log_p[k] - jnp.log(total)), 0.0))
    return alphas


def first_columns(frame, p0, p1, p2, p3, scores, log_out, out, spread_out, gathered):
    n_s = frame[N_S : N_S + 1, :]
    parts = (p0, p1, p2, p3)
    log_p = [jnp.log(part[4:5, :] / n_s) for part in parts]
    for k in range(ROW_BLOCKS):
        log_out[k : k + 1, :] = log_p[k]
    column_pass(frame, new_alphas(frame, parts, log_p), scores, out, spread_out, gathered)


def last_columns(
    frame, log_p, p0, p1, p2, p3, scores, weights, alpha_out, out, spread_out, gathered
):
    n_s = frame[N_S : N_S + 1, :]
    log_rows = [log_p[k : k + 1, :] for k in range(ROW_BLOCKS)]
    alphas = new_alphas(frame, (p0, p1, p2, p3), log_rows)
    alpha_out[...] = alphas[0]
    for k in range(ROW_BLOCKS):
        present = frame[ROWS_AT + k : ROWS_AT + k + 1, :]
        weights[k : k + 1, :] = present * n_s * jnp.exp(alphas[k])
    column_pass(frame, alphas, scores, out, spread_out, gathered)


def row_pass(frame, parts, scores, part, limits):
    n_t = frame[N_T : N_T + 1, :]
    total = jnp.sum(parts[...], axis=0)
    beta = TAU * (-jnp.log(n_t) - jnp.log(total))
    present = frame[COLUMNS_AT : COLUMNS_AT + COLUMN_BLOCKS, :] > 0.0
    limits[...] = jnp.where(present, beta * LOG2E, ABSENT)

    @pl.loop(0, ROWS // STRIP)
    def _(number):
        at = pl.ds(pl.multiple_of(number * STRIP, STRIP), STRIP)
        running = jnp.exp2(limits[0:1, :] - scores[0, at, :])
        for i in range(1, COLUMN_BLOCKS):
            running = running + jnp.exp2(limits[i : i + 1, :] - scores[i, at, :])
        part[at, :] = running

    return jnp.where(present, beta, 0.0)


def second_rows(frame, parts, scores, sums, part, limits):
    row_pass(frame, parts, scores, part, limits)
    for k in range(ROW_BLOCKS):
        sums[k : k + 1, :] = lane_sums(part, k)


def last_rows(frame, parts, scores, weights, beta_out, q0, q1, q2, q3, part, limits, betas):
    betas[...] = row_pass(frame, parts, scores, part, limits)
    place = lax.axis_index("x") * 4 + lax.axis_index("y")
    beta_out[...] = betas[pl.ds(place, 1), :]
    for k, out in enumerate((q0, q1, q2, q3)):
        present = frame[ROWS_AT + k : ROWS_AT + k + 1, :] > 0.0
        out[...] = jnp.where(present, weights[k : k + 1, :] * lane_sums(part, k), 0.0)


def outputs(alpha, beta, q0, q1, q2, q3, alpha_out, beta_out, mass_out):
    alpha_out[...] = alpha[...]
    beta_out[...] = beta[...]
    mass_out[...] = (q0[...] + q1[...]) + (q2[...] + q3[...])


def in_hbm(array):
    return pltpu.with_memory_space_constraint(array, pltpu.HBM)


def swapped(value, axis):
    return lax.ppermute(value, axis, [(0, 1), (1, 0)])


def across(value, k):
    return lax.ppermute(value, ROW_AXES, [(d, d ^ k) for d in range(4)])


def back(value, k):
    moves = [(z * 4 + g, (z ^ k) * 4 + (g - 1) % 4) for z in range(2) for g in range(4)]
    return lax.ppermute(value, ("z", "g"), moves)


def exchanged(copies):
    return lax.all_to_all(copies, COLUMN_AXES, split_axis=0, concat_axis=0, tiled=True)


def local(features, last_features, growth, cell_counts):
    part = pltpu.VMEM((ROWS, CELLS), F32)
    limits = pltpu.VMEM((COLUMN_BLOCKS, CELLS), F32)
    some_cells = shape(CELLS, WIDTH, dtype=BF16)
    row_parts = shape(8, CELLS)
    column_parts = shape(COLUMN_BLOCKS, COLUMN_BLOCKS, CELLS)

    with jax.named_scope("moments"):
        message, own, last, frame = call(
            local_sums,
            (row_parts, some_cells, some_cells, shape(FRAME, CELLS)),
            4,
            (
                pltpu.VMEM((1, CELLS, WIDTH), BF16),
                pltpu.VMEM((CELLS, WIDTH), BF16),
                pltpu.VMEM((1, CELLS), F32),
                pltpu.SMEM((5,), jnp.int32),
                pltpu.SemaphoreType.DMA((4,)),
            ),
            space=pltpu.HBM,
            name="local_sums",
        )(*(in_hbm(a) for a in (features, last_features, growth, cell_counts)))
        shifted = back(own, 0)
        other = swapped(message, "c")
        mine, near = call(
            core_sums, (row_parts, shape(2 * CELLS, WIDTH, dtype=BF16)), 4, name="core_sums"
        )(message, other, own, swapped(own, "c"))
    with jax.named_scope("gather"):
        sums = (swapped(mine, "z"), back(mine, 0), back(mine, 1))
        far = swapped(near, "z")
        copies = call(
            parcel, shape(COLUMN_BLOCKS, CELLS + EXTRA, WIDTH, dtype=BF16), 7, awaited=1, name="parcel"
        )(frame, mine, *sums, shifted, last, far)
        targets = exchanged(copies)

    def row_exchange(sums):
        return [sums] + [across(sums, k) for k in range(1, ROW_BLOCKS)]

    with jax.named_scope("first_rows"):
        scores, sums = call(
            first_pass,
            (shape(COLUMN_BLOCKS, ROWS, CELLS), row_parts),
            4,
            (pltpu.VMEM((ROWS, WIDTH), BF16), part, part, limits, limits),
            name="first_pass",
        )(frame, targets, near, far)
    with jax.named_scope("first_columns"):
        log_p, copies = call(
            first_columns,
            (shape(ROW_BLOCKS, CELLS), column_parts),
            6,
            (part, limits),
            name="first_columns",
        )(frame, *row_exchange(sums), scores)
        parts = exchanged(copies)
    with jax.named_scope("second_rows"):
        sums = call(second_rows, shape(ROW_BLOCKS, CELLS), 3, (part, limits), name="second_rows")(
            frame, parts, scores
        )
    with jax.named_scope("last_columns"):
        weights, source_pot, copies = call(
            last_columns,
            (shape(ROW_BLOCKS, CELLS), shape(1, CELLS), column_parts),
            7,
            (part, limits),
            name="last_columns",
        )(frame, log_p, *row_exchange(sums), scores)
        parts = exchanged(copies)
    with jax.named_scope("mass"):
        target_pot, *masses = call(
            last_rows, (shape(1, CELLS),) * 5, 4, (part, limits, limits), name="last_rows"
        )(frame, parts, scores, weights)
        masses = [masses[0]] + [across(masses[k], k) for k in range(1, ROW_BLOCKS)]
        return call(outputs, (shape(1, CELLS),) * 3, 6, name="outputs")(
            source_pot, target_pot, *masses
        )


def solution(mesh):
    fine = Mesh(mesh.devices.reshape(SIZES), AXES)
    blk = ("x", "z", "y", "c")
    return jax.shard_map(
        local,
        mesh=fine,
        in_specs=(P("g", blk, None), P(blk, None), P("g", blk), P()),
        out_specs=(P("g", blk),) * 3,
        check_vma=False,
    )
```

```python
import math

import jax
import jax.numpy as jnp
from jax import lax
from jax.experimental import pallas as pl
from jax.experimental.pallas import tpu as pltpu
from jax.sharding import Mesh
from jax.sharding import PartitionSpec as P

AXES = ("x", "z", "y", "c", "g")
SIZES = (4, 2, 4, 2, 4)
ROW_AXES = ("z", "c")
COLUMN_AXES = ("x", "y")

EPSILON = 0.1
PENALTY = 1.0
TAU = PENALTY / (PENALTY + EPSILON)
LOG2E = math.log2(math.e)
ABSENT = -1e30

CELLS = 128
WIDTH = 256
ROW_BLOCKS = 4
COLUMN_BLOCKS = 16
ROWS = ROW_BLOCKS * CELLS
STRIP = 64

COLUMNS_AT = 0
ROWS_AT = 16
N_S = 20
N_T = 21
GROWTH = 22
LAST_GROUP = 23
FRAME = 24

F32 = jnp.float32
BF16 = jnp.bfloat16


def shape(*dims, dtype=F32):
    return jax.ShapeDtypeStruct(dims, dtype)


def call(kernel, out_shape, n_inputs, scratch=(), space=pltpu.VMEM, name=None):
    return pl.pallas_call(
        kernel,
        out_shape=out_shape,
        in_specs=[pl.BlockSpec(memory_space=space)] * n_inputs,
        out_specs=jax.tree.map(lambda _: pl.BlockSpec(memory_space=pltpu.VMEM), out_shape),
        scratch_shapes=list(scratch),
        compiler_params=pltpu.CompilerParams(vmem_limit_bytes=16 * 1024 * 1024),
        name=name,
    )


def block_start(x, z, y, c):
    return (((x * 2 + z) * 4 + y) * 2 + c) * CELLS


def own_sums(cells, present):
    kept = jnp.where(present, cells, 0.0)
    total = jnp.sum(kept, axis=0, keepdims=True)
    squares = kept * kept
    norm = jnp.sum(jnp.sum(squares, axis=0, keepdims=True), axis=1, keepdims=True)
    squares = cells * cells
    norms = jnp.sum((squares[:, :CELLS] + squares[:, CELLS:]).T, axis=0, keepdims=True)
    return total[:, :CELLS], total[:, CELLS:], jnp.broadcast_to(norm, (1, CELLS)), norms


def local_sums(
    features, last, growth, counts, copies, own_out, last_out, frame, own, final, rates, numbers, sems
):
    loads = [
        pltpu.make_async_copy(source, target, sems.at[i])
        for i, (source, target) in enumerate(
            ((features, own), (last, final), (growth, rates), (counts, numbers))
        )
    ]
    for load in loads:
        load.start()
    x, z, y, c, g = (lax.axis_index(a) for a in AXES)
    start = block_start(x, z, y, c)
    for load in reversed(loads):
        load.wait()
    count_source = numbers[g]
    count_target = numbers[g + 1]
    row = start + lax.broadcasted_iota(jnp.int32, (CELLS, 1), 0)
    rows = own_sums(own[0].astype(F32), row < count_source)
    rows += own_sums(final[...].astype(F32), row < numbers[4])
    copies[...] = jnp.broadcast_to(jnp.concatenate(rows, axis=0)[None], copies.shape)
    own_out[...] = own[0]
    last_out[...] = final[...]
    block = lax.broadcasted_iota(jnp.int32, (COLUMN_BLOCKS, CELLS), 0)
    lane = lax.broadcasted_iota(jnp.int32, (COLUMN_BLOCKS, CELLS), 1)
    target = block_start(block >> 2, z, block & 3, c) + lane
    frame[COLUMNS_AT : COLUMNS_AT + COLUMN_BLOCKS, :] = jnp.where(target < count_target, 1.0, 0.0)
    for k in range(ROW_BLOCKS):
        place = (z * 2 + c) ^ k
        source = block_start(x, place >> 1, y, place & 1) + lane[:1]
        frame[ROWS_AT + k : ROWS_AT + k + 1, :] = jnp.where(source < count_source, 1.0, 0.0)
    ones = jnp.ones((1, CELLS), F32)
    frame[N_S : N_S + 1, :] = ones * count_source.astype(F32)
    frame[N_T : N_T + 1, :] = ones * count_target.astype(F32)
    frame[GROWTH : GROWTH + 1, :] = rates[...]
    frame[LAST_GROUP : LAST_GROUP + 1, :] = ones * (g == 3).astype(F32)


def group_sums(frame, messages, shifted, last, own, sums, norms, last_norms, own_out, copies):
    is_last = frame[LAST_GROUP : LAST_GROUP + 1, :] > 0.0
    wide_last = jnp.concatenate([is_last, is_last], axis=1)
    targets = jnp.where(wide_last, last[...].astype(F32), shifted[...].astype(F32)).astype(BF16)
    for i in range(COLUMN_BLOCKS):
        copies[i] = targets
    sums[...] = jnp.sum(messages[...], axis=0)
    for i in range(COLUMN_BLOCKS):
        norms[i : i + 1, :] = messages[i, 3:4, :]
        last_norms[i : i + 1, :] = messages[i, 7:8, :]
    own_out[...] = own[...]


def core_sums(mine, other, out):
    out[...] = mine[...] + other[...]


def prepared(
    frame, mine, across, back, back_across, norms, last_norms, x0, x1, x2, x3,
    rows, weights, column_weights, twice,
):
    is_last = frame[LAST_GROUP : LAST_GROUP + 1, :] > 0.0
    sources = mine[...] + across[...]
    targets = jnp.where(is_last, sources[4:8], (back[...] + back_across[...])[0:4])
    n_s = frame[N_S : N_S + 1, :]
    n_t = frame[N_T : N_T + 1, :]
    products = (sources[0:2] / n_s) * (targets[0:2] / n_t)
    dot = jnp.sum(jnp.sum(products, axis=0, keepdims=True), axis=1, keepdims=True)
    spread = sources[2:3] / n_s + targets[2:3] / n_t - 2.0 * dot
    scale = LOG2E / (EPSILON * spread)
    twice[...] = jnp.broadcast_to(2.0 * scale, twice.shape)
    column_weights[...] = jnp.where(is_last, last_norms[...], norms[...]) * scale
    for k, block in enumerate((x0[...], x1[...], x2[...], x3[...])):
        at = slice(k * CELLS, (k + 1) * CELLS)
        rows[at, :] = block
        wide = block.astype(F32)
        weights[at, :] = jnp.sum(wide * wide, axis=1, keepdims=True) * scale


def lane_sums(part, k):
    return jnp.sum(part[k * CELLS : (k + 1) * CELLS, :].T, axis=0, keepdims=True)


def first_pass(
    frame, targets, rows, weights, column_weights, twice, scores, sums, part, limits
):
    part[...] = jnp.zeros_like(part)
    limits[...] = jnp.where(frame[COLUMNS_AT : COLUMNS_AT + COLUMN_BLOCKS, :] > 0.0, 0.0, ABSENT)
    factor = twice[0:1, :]

    @pl.loop(0, COLUMN_BLOCKS // 2)
    def _(pair):
        first = pair * 2
        block = targets[pl.ds(first, 2)].reshape(2 * CELLS, WIDTH)
        products = lax.dot_general(
            rows[...], block, (((1,), (1,)), ((), ())), preferred_element_type=F32
        )
        running = part[...]
        for half in range(2):
            at = pl.ds(first + half, 1)
            tile = (weights[...] + column_weights[at, :]) - factor * products[
                :, half * CELLS : (half + 1) * CELLS
            ]
            scores[first + half] = tile
            running = running + jnp.exp2(limits[at, :] - tile)
        part[...] = running

    for k in range(ROW_BLOCKS):
        sums[k : k + 1, :] = lane_sums(part, k)
    sums[4:5, :] = frame[GROWTH : GROWTH + 1, :]
    sums[5:8, :] = jnp.zeros((3, CELLS), F32)


def column_pass(frame, alpha, scores, out, spread_out, gathered):
    for k in range(ROW_BLOCKS):
        present = frame[ROWS_AT + k : ROWS_AT + k + 1, :] > 0.0
        limit = jnp.where(present, alpha[k] * LOG2E, ABSENT)
        spread_out[k * CELLS : (k + 1) * CELLS, :] = jnp.broadcast_to(limit, (CELLS, CELLS)).T

    def strip(number, running):
        at = pl.ds(pl.multiple_of(number * STRIP, STRIP), STRIP)
        limit = spread_out[at, :]
        more = []
        for i, total in enumerate(running):
            terms = jnp.exp2(limit - scores[i, at, :])
            more.append(total + jnp.sum(terms.reshape(STRIP // 8, 8, CELLS), axis=0))
        return tuple(more)

    zeros = (jnp.zeros((8, CELLS), F32),) * COLUMN_BLOCKS
    for i, total in enumerate(lax.fori_loop(0, ROWS // STRIP, strip, zeros)):
        gathered[i : i + 1, :] = jnp.sum(total, axis=0, keepdims=True)
    out[...] = jnp.broadcast_to(gathered[...][None], out.shape)


def new_alphas(frame, parts, log_p):
    alphas = []
    for k in range(ROW_BLOCKS):
        total = parts[0][k : k + 1, :]
        for j in range(1, ROW_BLOCKS):
            total = total + parts[j][(k ^ j) : (k ^ j) + 1, :]
        present = frame[ROWS_AT + k : ROWS_AT + k + 1, :] > 0.0
        alphas.append(jnp.where(present, TAU * (log_p[k] - jnp.log(total)), 0.0))
    return alphas


def first_columns(frame, p0, p1, p2, p3, scores, log_out, out, spread_out, gathered):
    n_s = frame[N_S : N_S + 1, :]
    parts = (p0, p1, p2, p3)
    log_p = [jnp.log(part[4:5, :] / n_s) for part in parts]
    for k in range(ROW_BLOCKS):
        log_out[k : k + 1, :] = log_p[k]
    column_pass(frame, new_alphas(frame, parts, log_p), scores, out, spread_out, gathered)


def last_columns(
    frame, log_p, p0, p1, p2, p3, scores, weights, alpha_out, out, spread_out, gathered
):
    n_s = frame[N_S : N_S + 1, :]
    log_rows = [log_p[k : k + 1, :] for k in range(ROW_BLOCKS)]
    alphas = new_alphas(frame, (p0, p1, p2, p3), log_rows)
    alpha_out[...] = alphas[0]
    for k in range(ROW_BLOCKS):
        present = frame[ROWS_AT + k : ROWS_AT + k + 1, :]
        weights[k : k + 1, :] = present * n_s * jnp.exp(alphas[k])
    column_pass(frame, alphas, scores, out, spread_out, gathered)


def row_pass(frame, parts, scores, part, limits):
    n_t = frame[N_T : N_T + 1, :]
    total = jnp.sum(parts[...], axis=0)
    beta = TAU * (-jnp.log(n_t) - jnp.log(total))
    present = frame[COLUMNS_AT : COLUMNS_AT + COLUMN_BLOCKS, :] > 0.0
    limits[...] = jnp.where(present, beta * LOG2E, ABSENT)

    @pl.loop(0, ROWS // STRIP)
    def _(number):
        at = pl.ds(pl.multiple_of(number * STRIP, STRIP), STRIP)
        running = jnp.exp2(limits[0:1, :] - scores[0, at, :])
        for i in range(1, COLUMN_BLOCKS):
            running = running + jnp.exp2(limits[i : i + 1, :] - scores[i, at, :])
        part[at, :] = running

    return jnp.where(present, beta, 0.0)


def second_rows(frame, parts, scores, sums, part, limits):
    row_pass(frame, parts, scores, part, limits)
    for k in range(ROW_BLOCKS):
        sums[k : k + 1, :] = lane_sums(part, k)


def last_rows(frame, parts, scores, weights, beta_out, q0, q1, q2, q3, part, limits, betas):
    betas[...] = row_pass(frame, parts, scores, part, limits)
    place = lax.axis_index("x") * 4 + lax.axis_index("y")
    beta_out[...] = betas[pl.ds(place, 1), :]
    for k, out in enumerate((q0, q1, q2, q3)):
        present = frame[ROWS_AT + k : ROWS_AT + k + 1, :] > 0.0
        out[...] = jnp.where(present, weights[k : k + 1, :] * lane_sums(part, k), 0.0)


def outputs(alpha, beta, q0, q1, q2, q3, alpha_out, beta_out, mass_out):
    alpha_out[...] = alpha[...]
    beta_out[...] = beta[...]
    mass_out[...] = (q0[...] + q1[...]) + (q2[...] + q3[...])


def in_hbm(array):
    return pltpu.with_memory_space_constraint(array, pltpu.HBM)


def swapped(value, axis):
    return lax.ppermute(value, axis, [(0, 1), (1, 0)])


def across(value, k):
    return lax.ppermute(value, ROW_AXES, [(d, d ^ k) for d in range(4)])


def back(value, k):
    moves = [(z * 4 + g, (z ^ k) * 4 + (g - 1) % 4) for z in range(2) for g in range(4)]
    return lax.ppermute(value, ("z", "g"), moves)


def exchanged(copies):
    return lax.all_to_all(copies, COLUMN_AXES, split_axis=0, concat_axis=0, tiled=True)


def local(features, last_features, growth, cell_counts):
    part = pltpu.VMEM((ROWS, CELLS), F32)
    limits = pltpu.VMEM((COLUMN_BLOCKS, CELLS), F32)
    some_cells = shape(CELLS, WIDTH, dtype=BF16)
    row_parts = shape(8, CELLS)
    column_parts = shape(COLUMN_BLOCKS, COLUMN_BLOCKS, CELLS)

    with jax.named_scope("moments"):
        copies, own, last, frame = call(
            local_sums,
            (shape(COLUMN_BLOCKS, 8, CELLS), some_cells, some_cells, shape(FRAME, CELLS)),
            4,
            (
                pltpu.VMEM((1, CELLS, WIDTH), BF16),
                pltpu.VMEM((CELLS, WIDTH), BF16),
                pltpu.VMEM((1, CELLS), F32),
                pltpu.SMEM((5,), jnp.int32),
                pltpu.SemaphoreType.DMA((4,)),
            ),
            space=pltpu.HBM,
            name="local_sums",
        )(*(in_hbm(a) for a in (features, last_features, growth, cell_counts)))
        shifted = back(own, 0)
        every_norm = shape(COLUMN_BLOCKS, CELLS)
        sums, norms, last_norms, own, copies = call(
            group_sums,
            (row_parts, every_norm, every_norm, some_cells, shape(COLUMN_BLOCKS, CELLS, WIDTH, dtype=BF16)),
            5,
            name="group_sums",
        )(frame, exchanged(copies), shifted, last, own)
    with jax.named_scope("gather"):
        targets = exchanged(copies)
        sources = [own] + [across(own, k) for k in range(1, ROW_BLOCKS)]
        mine = call(core_sums, row_parts, 2, name="core_sums")(sums, swapped(sums, "c"))
        sums = (mine, swapped(mine, "z"), back(mine, 0), back(mine, 1))
        ready = call(
            prepared,
            (shape(ROWS, WIDTH, dtype=BF16), shape(ROWS, CELLS), every_norm, shape(8, CELLS)),
            11,
            name="prepared",
        )(frame, *sums, back(norms, 0), last_norms, *sources)

    def row_exchange(sums):
        return [sums] + [across(sums, k) for k in range(1, ROW_BLOCKS)]

    with jax.named_scope("first_rows"):
        scores, sums = call(
            first_pass,
            (shape(COLUMN_BLOCKS, ROWS, CELLS), row_parts),
            6,
            (part, limits),
            name="first_pass",
        )(frame, targets, *ready)
    with jax.named_scope("first_columns"):
        log_p, copies = call(
            first_columns,
            (shape(ROW_BLOCKS, CELLS), column_parts),
            6,
            (part, limits),
            name="first_columns",
        )(frame, *row_exchange(sums), scores)
        parts = exchanged(copies)
    with jax.named_scope("second_rows"):
        sums = call(second_rows, shape(ROW_BLOCKS, CELLS), 3, (part, limits), name="second_rows")(
            frame, parts, scores
        )
    with jax.named_scope("last_columns"):
        weights, source_pot, copies = call(
            last_columns,
            (shape(ROW_BLOCKS, CELLS), shape(1, CELLS), column_parts),
            7,
            (part, limits),
            name="last_columns",
        )(frame, log_p, *row_exchange(sums), scores)
        parts = exchanged(copies)
    with jax.named_scope("mass"):
        target_pot, *masses = call(
            last_rows, (shape(1, CELLS),) * 5, 4, (part, limits, limits), name="last_rows"
        )(frame, parts, scores, weights)
        masses = [masses[0]] + [across(masses[k], k) for k in range(1, ROW_BLOCKS)]
        return call(outputs, (shape(1, CELLS),) * 3, 6, name="outputs")(
            source_pot, target_pot, *masses
        )


def solution(mesh):
    fine = Mesh(mesh.devices.reshape(SIZES), AXES)
    blk = ("x", "z", "y", "c")
    return jax.shard_map(
        local,
        mesh=fine,
        in_specs=(P("g", blk, None), P(blk, None), P("g", blk), P()),
        out_specs=(P("g", blk),) * 3,
        check_vma=False,
    )
```

```python
import math

import jax
import jax.numpy as jnp
from jax import lax
from jax.experimental import pallas as pl
from jax.experimental.pallas import tpu as pltpu
from jax.sharding import Mesh
from jax.sharding import PartitionSpec as P

AXES = ("x", "z", "y", "c", "g")
SIZES = (4, 2, 4, 2, 4)
ROW_AXES = ("z", "c")
COLUMN_AXES = ("x", "y")

EPSILON = 0.1
PENALTY = 1.0
TAU = PENALTY / (PENALTY + EPSILON)
LOG2E = math.log2(math.e)
ABSENT = -1e30

CELLS = 128
WIDTH = 256
ROW_BLOCKS = 4
COLUMN_BLOCKS = 16
ROWS = ROW_BLOCKS * CELLS
STRIP = 64

COLUMNS_AT = 0
ROWS_AT = 16
N_S = 20
N_T = 21
GROWTH = 22
LAST_GROUP = 23
FRAME = 24

F32 = jnp.float32
BF16 = jnp.bfloat16


def shape(*dims, dtype=F32):
    return jax.ShapeDtypeStruct(dims, dtype)


def call(kernel, out_shape, n_inputs, scratch=(), space=pltpu.VMEM, awaited=0, name=None):
    return pl.pallas_call(
        kernel,
        out_shape=out_shape,
        in_specs=[pl.BlockSpec(memory_space=space)] * n_inputs
        + [pl.BlockSpec(memory_space=pl.ANY)] * awaited,
        out_specs=jax.tree.map(lambda _: pl.BlockSpec(memory_space=pltpu.VMEM), out_shape),
        scratch_shapes=list(scratch),
        compiler_params=pltpu.CompilerParams(vmem_limit_bytes=16 * 1024 * 1024),
        name=name,
    )


def block_start(x, z, y, c):
    return (((x * 2 + z) * 4 + y) * 2 + c) * CELLS


def own_sums(cells, present):
    kept = jnp.where(present, cells, 0.0)
    total = jnp.sum(kept, axis=0, keepdims=True)
    squares = kept * kept
    norm = jnp.sum(jnp.sum(squares, axis=0, keepdims=True), axis=1, keepdims=True)
    squares = cells * cells
    norms = jnp.sum((squares[:, :CELLS] + squares[:, CELLS:]).T, axis=0, keepdims=True)
    return total[:, :CELLS], total[:, CELLS:], jnp.broadcast_to(norm, (1, CELLS)), norms


def local_sums(
    features, last, growth, counts, copies, own_out, last_out, frame, own, final, rates, numbers, sems
):
    loads = [
        pltpu.make_async_copy(source, target, sems.at[i])
        for i, (source, target) in enumerate(
            ((features, own), (last, final), (growth, rates), (counts, numbers))
        )
    ]
    for load in loads:
        load.start()
    x, z, y, c, g = (lax.axis_index(a) for a in AXES)
    start = block_start(x, z, y, c)
    for load in reversed(loads):
        load.wait()
    count_source = numbers[g]
    count_target = numbers[g + 1]
    row = start + lax.broadcasted_iota(jnp.int32, (CELLS, 1), 0)
    rows = own_sums(own[0].astype(F32), row < count_source)
    rows += own_sums(final[...].astype(F32), row < numbers[4])
    copies[...] = jnp.broadcast_to(jnp.concatenate(rows, axis=0)[None], copies.shape)
    own_out[...] = own[0]
    last_out[...] = final[...]
    block = lax.broadcasted_iota(jnp.int32, (COLUMN_BLOCKS, CELLS), 0)
    lane = lax.broadcasted_iota(jnp.int32, (COLUMN_BLOCKS, CELLS), 1)
    target = block_start(block >> 2, z, block & 3, c) + lane
    frame[COLUMNS_AT : COLUMNS_AT + COLUMN_BLOCKS, :] = jnp.where(target < count_target, 1.0, 0.0)
    for k in range(ROW_BLOCKS):
        place = (z * 2 + c) ^ k
        source = block_start(x, place >> 1, y, place & 1) + lane[:1]
        frame[ROWS_AT + k : ROWS_AT + k + 1, :] = jnp.where(source < count_source, 1.0, 0.0)
    ones = jnp.ones((1, CELLS), F32)
    frame[N_S : N_S + 1, :] = ones * count_source.astype(F32)
    frame[N_T : N_T + 1, :] = ones * count_target.astype(F32)
    frame[GROWTH : GROWTH + 1, :] = rates[...]
    frame[LAST_GROUP : LAST_GROUP + 1, :] = ones * (g == 3).astype(F32)


def group_sums(frame, messages, shifted, last, x1, x2, x3, sums, norms, last_norms, copies):
    is_last = frame[LAST_GROUP : LAST_GROUP + 1, :] > 0.0
    wide_last = jnp.concatenate([is_last, is_last], axis=1)
    targets = jnp.where(wide_last, last[...].astype(F32), shifted[...].astype(F32)).astype(BF16)
    for i in range(COLUMN_BLOCKS):
        copies[i] = targets
    sums[...] = jnp.sum(messages[...], axis=0)
    for i in range(COLUMN_BLOCKS):
        norms[i : i + 1, :] = messages[i, 3:4, :]
        last_norms[i : i + 1, :] = messages[i, 7:8, :]


def core_sums(mine, other, out):
    out[...] = mine[...] + other[...]


def prepared(
    frame, mine, across, back, back_across, norms, last_norms, x0, x1, x2, x3,
    rows, weights, column_weights, twice,
):
    is_last = frame[LAST_GROUP : LAST_GROUP + 1, :] > 0.0
    sources = mine[...] + across[...]
    targets = jnp.where(is_last, sources[4:8], (back[...] + back_across[...])[0:4])
    n_s = frame[N_S : N_S + 1, :]
    n_t = frame[N_T : N_T + 1, :]
    products = (sources[0:2] / n_s) * (targets[0:2] / n_t)
    dot = jnp.sum(jnp.sum(products, axis=0, keepdims=True), axis=1, keepdims=True)
    spread = sources[2:3] / n_s + targets[2:3] / n_t - 2.0 * dot
    scale = LOG2E / (EPSILON * spread)
    twice[...] = jnp.broadcast_to(2.0 * scale, twice.shape)
    column_weights[...] = jnp.where(is_last, last_norms[...], norms[...]) * scale
    for k, block in enumerate((x0[...], x1[...], x2[...], x3[...])):
        at = slice(k * CELLS, (k + 1) * CELLS)
        rows[at, :] = block
        wide = block.astype(F32)
        weights[at, :] = jnp.sum(wide * wide, axis=1, keepdims=True) * scale


def lane_sums(part, k):
    return jnp.sum(part[k * CELLS : (k + 1) * CELLS, :].T, axis=0, keepdims=True)


def first_pass(
    frame, targets, rows, weights, column_weights, twice, scores, sums, part, limits
):
    part[...] = jnp.zeros_like(part)
    limits[...] = jnp.where(frame[COLUMNS_AT : COLUMNS_AT + COLUMN_BLOCKS, :] > 0.0, 0.0, ABSENT)
    factor = twice[0:1, :]

    @pl.loop(0, COLUMN_BLOCKS // 2)
    def _(pair):
        first = pair * 2
        block = targets[pl.ds(first, 2)].reshape(2 * CELLS, WIDTH)
        products = lax.dot_general(
            rows[...], block, (((1,), (1,)), ((), ())), preferred_element_type=F32
        )
        running = part[...]
        for half in range(2):
            at = pl.ds(first + half, 1)
            tile = (weights[...] + column_weights[at, :]) - factor * products[
                :, half * CELLS : (half + 1) * CELLS
            ]
            scores[first + half] = tile
            running = running + jnp.exp2(limits[at, :] - tile)
        part[...] = running

    for k in range(ROW_BLOCKS):
        sums[k : k + 1, :] = lane_sums(part, k)
    sums[4:5, :] = frame[GROWTH : GROWTH + 1, :]
    sums[5:8, :] = jnp.zeros((3, CELLS), F32)


def column_pass(frame, alpha, scores, out, spread_out, gathered):
    for k in range(ROW_BLOCKS):
        present = frame[ROWS_AT + k : ROWS_AT + k + 1, :] > 0.0
        limit = jnp.where(present, alpha[k] * LOG2E, ABSENT)
        spread_out[k * CELLS : (k + 1) * CELLS, :] = jnp.broadcast_to(limit, (CELLS, CELLS)).T

    def strip(number, running):
        at = pl.ds(pl.multiple_of(number * STRIP, STRIP), STRIP)
        limit = spread_out[at, :]
        more = []
        for i, total in enumerate(running):
            terms = jnp.exp2(limit - scores[i, at, :])
            more.append(total + jnp.sum(terms.reshape(STRIP // 8, 8, CELLS), axis=0))
        return tuple(more)

    zeros = (jnp.zeros((8, CELLS), F32),) * COLUMN_BLOCKS
    for i, total in enumerate(lax.fori_loop(0, ROWS // STRIP, strip, zeros)):
        gathered[i : i + 1, :] = jnp.sum(total, axis=0, keepdims=True)
    out[...] = jnp.broadcast_to(gathered[...][None], out.shape)


def new_alphas(frame, parts, log_p):
    alphas = []
    for k in range(ROW_BLOCKS):
        total = parts[0][k : k + 1, :]
        for j in range(1, ROW_BLOCKS):
            total = total + parts[j][(k ^ j) : (k ^ j) + 1, :]
        present = frame[ROWS_AT + k : ROWS_AT + k + 1, :] > 0.0
        alphas.append(jnp.where(present, TAU * (log_p[k] - jnp.log(total)), 0.0))
    return alphas


def first_columns(frame, p0, p1, p2, p3, scores, log_out, out, spread_out, gathered):
    n_s = frame[N_S : N_S + 1, :]
    parts = (p0, p1, p2, p3)
    log_p = [jnp.log(part[4:5, :] / n_s) for part in parts]
    for k in range(ROW_BLOCKS):
        log_out[k : k + 1, :] = log_p[k]
    column_pass(frame, new_alphas(frame, parts, log_p), scores, out, spread_out, gathered)


def last_columns(
    frame, log_p, p0, p1, p2, p3, scores, weights, alpha_out, out, spread_out, gathered
):
    n_s = frame[N_S : N_S + 1, :]
    log_rows = [log_p[k : k + 1, :] for k in range(ROW_BLOCKS)]
    alphas = new_alphas(frame, (p0, p1, p2, p3), log_rows)
    alpha_out[...] = alphas[0]
    for k in range(ROW_BLOCKS):
        present = frame[ROWS_AT + k : ROWS_AT + k + 1, :]
        weights[k : k + 1, :] = present * n_s * jnp.exp(alphas[k])
    column_pass(frame, alphas, scores, out, spread_out, gathered)


def row_pass(frame, parts, scores, part, limits):
    n_t = frame[N_T : N_T + 1, :]
    total = jnp.sum(parts[...], axis=0)
    beta = TAU * (-jnp.log(n_t) - jnp.log(total))
    present = frame[COLUMNS_AT : COLUMNS_AT + COLUMN_BLOCKS, :] > 0.0
    limits[...] = jnp.where(present, beta * LOG2E, ABSENT)

    @pl.loop(0, ROWS // STRIP)
    def _(number):
        at = pl.ds(pl.multiple_of(number * STRIP, STRIP), STRIP)
        running = jnp.exp2(limits[0:1, :] - scores[0, at, :])
        for i in range(1, COLUMN_BLOCKS):
            running = running + jnp.exp2(limits[i : i + 1, :] - scores[i, at, :])
        part[at, :] = running

    return jnp.where(present, beta, 0.0)


def second_rows(frame, parts, scores, sums, part, limits):
    row_pass(frame, parts, scores, part, limits)
    for k in range(ROW_BLOCKS):
        sums[k : k + 1, :] = lane_sums(part, k)


def last_rows(frame, parts, scores, weights, beta_out, q0, q1, q2, q3, part, limits, betas):
    betas[...] = row_pass(frame, parts, scores, part, limits)
    place = lax.axis_index("x") * 4 + lax.axis_index("y")
    beta_out[...] = betas[pl.ds(place, 1), :]
    for k, out in enumerate((q0, q1, q2, q3)):
        present = frame[ROWS_AT + k : ROWS_AT + k + 1, :] > 0.0
        out[...] = jnp.where(present, weights[k : k + 1, :] * lane_sums(part, k), 0.0)


def outputs(alpha, beta, q0, q1, q2, q3, alpha_out, beta_out, mass_out):
    alpha_out[...] = alpha[...]
    beta_out[...] = beta[...]
    mass_out[...] = (q0[...] + q1[...]) + (q2[...] + q3[...])


def in_hbm(array):
    return pltpu.with_memory_space_constraint(array, pltpu.HBM)


def swapped(value, axis):
    return lax.ppermute(value, axis, [(0, 1), (1, 0)])


def across(value, k):
    return lax.ppermute(value, ROW_AXES, [(d, d ^ k) for d in range(4)])


def back(value, k):
    moves = [(z * 4 + g, (z ^ k) * 4 + (g - 1) % 4) for z in range(2) for g in range(4)]
    return lax.ppermute(value, ("z", "g"), moves)


def exchanged(copies):
    return lax.all_to_all(copies, COLUMN_AXES, split_axis=0, concat_axis=0, tiled=True)


def local(features, last_features, growth, cell_counts):
    part = pltpu.VMEM((ROWS, CELLS), F32)
    limits = pltpu.VMEM((COLUMN_BLOCKS, CELLS), F32)
    some_cells = shape(CELLS, WIDTH, dtype=BF16)
    row_parts = shape(8, CELLS)
    column_parts = shape(COLUMN_BLOCKS, COLUMN_BLOCKS, CELLS)

    with jax.named_scope("moments"):
        copies, own, last, frame = call(
            local_sums,
            (shape(COLUMN_BLOCKS, 8, CELLS), some_cells, some_cells, shape(FRAME, CELLS)),
            4,
            (
                pltpu.VMEM((1, CELLS, WIDTH), BF16),
                pltpu.VMEM((CELLS, WIDTH), BF16),
                pltpu.VMEM((1, CELLS), F32),
                pltpu.SMEM((5,), jnp.int32),
                pltpu.SemaphoreType.DMA((4,)),
            ),
            space=pltpu.HBM,
            name="local_sums",
        )(*(in_hbm(a) for a in (features, last_features, growth, cell_counts)))
        shifted = back(own, 0)
        every_norm = shape(COLUMN_BLOCKS, CELLS)
        sources = [across(own, k) for k in range(1, ROW_BLOCKS)]
        sums, norms, last_norms, copies = call(
            group_sums,
            (row_parts, every_norm, every_norm, shape(COLUMN_BLOCKS, CELLS, WIDTH, dtype=BF16)),
            4,
            awaited=3,
            name="group_sums",
        )(frame, exchanged(copies), shifted, last, *sources)
    with jax.named_scope("gather"):
        targets = exchanged(copies)
        mine = call(core_sums, row_parts, 2, name="core_sums")(sums, swapped(sums, "c"))
        sums = (mine, swapped(mine, "z"), back(mine, 0), back(mine, 1))
        ready = call(
            prepared,
            (shape(ROWS, WIDTH, dtype=BF16), shape(ROWS, CELLS), every_norm, shape(8, CELLS)),
            11,
            name="prepared",
        )(frame, *sums, back(norms, 0), last_norms, own, *sources)

    def row_exchange(sums):
        return [sums] + [across(sums, k) for k in range(1, ROW_BLOCKS)]

    with jax.named_scope("first_rows"):
        scores, sums = call(
            first_pass,
            (shape(COLUMN_BLOCKS, ROWS, CELLS), row_parts),
            6,
            (part, limits),
            name="first_pass",
        )(frame, targets, *ready)
    with jax.named_scope("first_columns"):
        log_p, copies = call(
            first_columns,
            (shape(ROW_BLOCKS, CELLS), column_parts),
            6,
            (part, limits),
            name="first_columns",
        )(frame, *row_exchange(sums), scores)
        parts = exchanged(copies)
    with jax.named_scope("second_rows"):
        sums = call(second_rows, shape(ROW_BLOCKS, CELLS), 3, (part, limits), name="second_rows")(
            frame, parts, scores
        )
    with jax.named_scope("last_columns"):
        weights, source_pot, copies = call(
            last_columns,
            (shape(ROW_BLOCKS, CELLS), shape(1, CELLS), column_parts),
            7,
            (part, limits),
            name="last_columns",
        )(frame, log_p, *row_exchange(sums), scores)
        parts = exchanged(copies)
    with jax.named_scope("mass"):
        target_pot, *masses = call(
            last_rows, (shape(1, CELLS),) * 5, 4, (part, limits, limits), name="last_rows"
        )(frame, parts, scores, weights)
        masses = [masses[0]] + [across(masses[k], k) for k in range(1, ROW_BLOCKS)]
        return call(outputs, (shape(1, CELLS),) * 3, 6, name="outputs")(
            source_pot, target_pot, *masses
        )


def solution(mesh):
    fine = Mesh(mesh.devices.reshape(SIZES), AXES)
    blk = ("x", "z", "y", "c")
    return jax.shard_map(
        local,
        mesh=fine,
        in_specs=(P("g", blk, None), P(blk, None), P("g", blk), P()),
        out_specs=(P("g", blk),) * 3,
        check_vma=False,
    )
```

```python
import math

import jax
import jax.numpy as jnp
from jax import lax
from jax.experimental import pallas as pl
from jax.experimental.pallas import tpu as pltpu
from jax.sharding import Mesh
from jax.sharding import PartitionSpec as P

AXES = ("x", "z", "y", "c", "g")
SIZES = (4, 2, 4, 2, 4)
ROW_AXES = ("z", "c")
COLUMN_AXES = ("x", "y")

EPSILON = 0.1
PENALTY = 1.0
TAU = PENALTY / (PENALTY + EPSILON)
LOG2E = math.log2(math.e)
ABSENT = -1e30

CELLS = 128
WIDTH = 256
ROW_BLOCKS = 4
COLUMN_BLOCKS = 16
ROWS = ROW_BLOCKS * CELLS
STRIP = 64

COLUMNS_AT = 0
ROWS_AT = 16
N_S = 20
N_T = 21
GROWTH = 22
LAST_GROUP = 23
FRAME = 24

F32 = jnp.float32
BF16 = jnp.bfloat16


def shape(*dims, dtype=F32):
    return jax.ShapeDtypeStruct(dims, dtype)


def call(kernel, out_shape, n_inputs, scratch=(), space=pltpu.VMEM, awaited=0, name=None):
    return pl.pallas_call(
        kernel,
        out_shape=out_shape,
        in_specs=[pl.BlockSpec(memory_space=space)] * n_inputs
        + [pl.BlockSpec(memory_space=pl.ANY)] * awaited,
        out_specs=jax.tree.map(lambda _: pl.BlockSpec(memory_space=pltpu.VMEM), out_shape),
        scratch_shapes=list(scratch),
        compiler_params=pltpu.CompilerParams(vmem_limit_bytes=16 * 1024 * 1024),
        name=name,
    )


def block_start(x, z, y, c):
    return (((x * 2 + z) * 4 + y) * 2 + c) * CELLS


def own_sums(cells, present):
    kept = jnp.where(present, cells, 0.0)
    total = jnp.sum(kept, axis=0, keepdims=True)
    squares = jnp.sum(kept * kept, axis=0, keepdims=True)
    norm = jnp.sum(squares, axis=1, keepdims=True)
    zeros = jnp.zeros((1, CELLS), F32)
    return total[:, :CELLS], total[:, CELLS:], jnp.broadcast_to(norm, (1, CELLS)), zeros


def local_sums(
    features, last, growth, counts, copies, own_out, last_out, frame, own, final, rates, numbers, sems
):
    loads = [
        pltpu.make_async_copy(source, target, sems.at[i])
        for i, (source, target) in enumerate(
            ((features, own), (last, final), (growth, rates), (counts, numbers))
        )
    ]
    for load in loads:
        load.start()
    x, z, y, c, g = (lax.axis_index(a) for a in AXES)
    start = block_start(x, z, y, c)
    for load in reversed(loads):
        load.wait()
    count_source = numbers[g]
    count_target = numbers[g + 1]
    row = start + lax.broadcasted_iota(jnp.int32, (CELLS, 1), 0)
    rows = own_sums(own[0].astype(F32), row < count_source)
    rows += own_sums(final[...].astype(F32), row < numbers[4])
    copies[...] = jnp.broadcast_to(jnp.concatenate(rows, axis=0)[None], copies.shape)
    own_out[...] = own[0]
    last_out[...] = final[...]
    block = lax.broadcasted_iota(jnp.int32, (COLUMN_BLOCKS, CELLS), 0)
    lane = lax.broadcasted_iota(jnp.int32, (COLUMN_BLOCKS, CELLS), 1)
    target = block_start(block >> 2, z, block & 3, c) + lane
    frame[COLUMNS_AT : COLUMNS_AT + COLUMN_BLOCKS, :] = jnp.where(target < count_target, 1.0, 0.0)
    for k in range(ROW_BLOCKS):
        place = (z * 2 + c) ^ k
        source = block_start(x, place >> 1, y, place & 1) + lane[:1]
        frame[ROWS_AT + k : ROWS_AT + k + 1, :] = jnp.where(source < count_source, 1.0, 0.0)
    ones = jnp.ones((1, CELLS), F32)
    frame[N_S : N_S + 1, :] = ones * count_source.astype(F32)
    frame[N_T : N_T + 1, :] = ones * count_target.astype(F32)
    frame[GROWTH : GROWTH + 1, :] = rates[...]
    frame[LAST_GROUP : LAST_GROUP + 1, :] = ones * (g == 3).astype(F32)


def parcel(frame, shifted, last, copies):
    is_last = frame[LAST_GROUP : LAST_GROUP + 1, :] > 0.0
    wide_last = jnp.concatenate([is_last, is_last], axis=1)
    targets = jnp.where(wide_last, last[...].astype(F32), shifted[...].astype(F32)).astype(BF16)
    for i in range(COLUMN_BLOCKS):
        copies[i] = targets


def group_sums(messages, own, other, copies, sums, near, copies_out):
    sums[...] = jnp.sum(messages[...], axis=0)
    near[:CELLS, :] = own[...]
    near[CELLS:, :] = other[...]


def core_sums(mine, other, out):
    out[...] = mine[...] + other[...]


def prepared(frame, mine, across, back, back_across, near, far, rows, weights, scales):
    is_last = frame[LAST_GROUP : LAST_GROUP + 1, :] > 0.0
    sources = mine[...] + across[...]
    targets = jnp.where(is_last, sources[4:8], (back[...] + back_across[...])[0:4])
    n_s = frame[N_S : N_S + 1, :]
    n_t = frame[N_T : N_T + 1, :]
    products = (sources[0:2] / n_s) * (targets[0:2] / n_t)
    dot = jnp.sum(jnp.sum(products, axis=0, keepdims=True), axis=1, keepdims=True)
    spread = sources[2:3] / n_s + targets[2:3] / n_t - 2.0 * dot
    scale = LOG2E / (EPSILON * spread)
    scales[...] = jnp.broadcast_to(scale, scales.shape)
    for k, block in enumerate((near[...], far[...])):
        at = slice(k * 2 * CELLS, (k + 1) * 2 * CELLS)
        rows[at, :] = block
        wide = block.astype(F32)
        weights[at, :] = jnp.sum(wide * wide, axis=1, keepdims=True) * scale


def lane_sums(part, k):
    return jnp.sum(part[k * CELLS : (k + 1) * CELLS, :].T, axis=0, keepdims=True)


def first_pass(frame, targets, rows, weights, scales, scores, sums, part, limits):
    part[...] = jnp.zeros_like(part)
    limits[...] = jnp.where(frame[COLUMNS_AT : COLUMNS_AT + COLUMN_BLOCKS, :] > 0.0, 0.0, ABSENT)
    scale = scales[0:1, :]
    twice = 2.0 * scale

    @pl.loop(0, COLUMN_BLOCKS // 2)
    def _(pair):
        first = pair * 2
        block = targets[pl.ds(first, 2)].reshape(2 * CELLS, WIDTH)
        products = lax.dot_general(
            rows[...], block, (((1,), (1,)), ((), ())), preferred_element_type=F32
        )
        running = part[...]
        for half in range(2):
            wide = targets[first + half].astype(F32)
            squares = wide * wide
            norms = jnp.sum((squares[:, :CELLS] + squares[:, CELLS:]).T, axis=0, keepdims=True)
            tile = (weights[...] + norms * scale) - twice * products[
                :, half * CELLS : (half + 1) * CELLS
            ]
            scores[first + half] = tile
            running = running + jnp.exp2(limits[pl.ds(first + half, 1), :] - tile)
        part[...] = running

    for k in range(ROW_BLOCKS):
        sums[k : k + 1, :] = lane_sums(part, k)
    sums[4:5, :] = frame[GROWTH : GROWTH + 1, :]
    sums[5:8, :] = jnp.zeros((3, CELLS), F32)


def column_pass(frame, alpha, scores, out, spread_out, gathered):
    for k in range(ROW_BLOCKS):
        present = frame[ROWS_AT + k : ROWS_AT + k + 1, :] > 0.0
        limit = jnp.where(present, alpha[k] * LOG2E, ABSENT)
        spread_out[k * CELLS : (k + 1) * CELLS, :] = jnp.broadcast_to(limit, (CELLS, CELLS)).T

    def strip(number, running):
        at = pl.ds(pl.multiple_of(number * STRIP, STRIP), STRIP)
        limit = spread_out[at, :]
        more = []
        for i, total in enumerate(running):
            terms = jnp.exp2(limit - scores[i, at, :])
            more.append(total + jnp.sum(terms.reshape(STRIP // 8, 8, CELLS), axis=0))
        return tuple(more)

    zeros = (jnp.zeros((8, CELLS), F32),) * COLUMN_BLOCKS
    for i, total in enumerate(lax.fori_loop(0, ROWS // STRIP, strip, zeros)):
        gathered[i : i + 1, :] = jnp.sum(total, axis=0, keepdims=True)
    out[...] = jnp.broadcast_to(gathered[...][None], out.shape)


def new_alphas(frame, parts, log_p):
    alphas = []
    for k in range(ROW_BLOCKS):
        total = parts[0][k : k + 1, :]
        for j in range(1, ROW_BLOCKS):
            total = total + parts[j][(k ^ j) : (k ^ j) + 1, :]
        present = frame[ROWS_AT + k : ROWS_AT + k + 1, :] > 0.0
        alphas.append(jnp.where(present, TAU * (log_p[k] - jnp.log(total)), 0.0))
    return alphas


def first_columns(frame, p0, p1, p2, p3, scores, log_out, out, spread_out, gathered):
    n_s = frame[N_S : N_S + 1, :]
    parts = (p0, p1, p2, p3)
    log_p = [jnp.log(part[4:5, :] / n_s) for part in parts]
    for k in range(ROW_BLOCKS):
        log_out[k : k + 1, :] = log_p[k]
    column_pass(frame, new_alphas(frame, parts, log_p), scores, out, spread_out, gathered)


def last_columns(
    frame, log_p, p0, p1, p2, p3, scores, weights, alpha_out, out, spread_out, gathered
):
    n_s = frame[N_S : N_S + 1, :]
    log_rows = [log_p[k : k + 1, :] for k in range(ROW_BLOCKS)]
    alphas = new_alphas(frame, (p0, p1, p2, p3), log_rows)
    alpha_out[...] = alphas[0]
    for k in range(ROW_BLOCKS):
        present = frame[ROWS_AT + k : ROWS_AT + k + 1, :]
        weights[k : k + 1, :] = present * n_s * jnp.exp(alphas[k])
    column_pass(frame, alphas, scores, out, spread_out, gathered)


def row_pass(frame, parts, scores, part, limits):
    n_t = frame[N_T : N_T + 1, :]
    total = jnp.sum(parts[...], axis=0)
    beta = TAU * (-jnp.log(n_t) - jnp.log(total))
    present = frame[COLUMNS_AT : COLUMNS_AT + COLUMN_BLOCKS, :] > 0.0
    limits[...] = jnp.where(present, beta * LOG2E, ABSENT)

    @pl.loop(0, ROWS // STRIP)
    def _(number):
        at = pl.ds(pl.multiple_of(number * STRIP, STRIP), STRIP)
        running = jnp.exp2(limits[0:1, :] - scores[0, at, :])
        for i in range(1, COLUMN_BLOCKS):
            running = running + jnp.exp2(limits[i : i + 1, :] - scores[i, at, :])
        part[at, :] = running

    return jnp.where(present, beta, 0.0)


def second_rows(frame, parts, scores, sums, part, limits):
    row_pass(frame, parts, scores, part, limits)
    for k in range(ROW_BLOCKS):
        sums[k : k + 1, :] = lane_sums(part, k)


def last_rows(frame, parts, scores, weights, beta_out, q0, q1, q2, q3, part, limits, betas):
    betas[...] = row_pass(frame, parts, scores, part, limits)
    place = lax.axis_index("x") * 4 + lax.axis_index("y")
    beta_out[...] = betas[pl.ds(place, 1), :]
    for k, out in enumerate((q0, q1, q2, q3)):
        present = frame[ROWS_AT + k : ROWS_AT + k + 1, :] > 0.0
        out[...] = jnp.where(present, weights[k : k + 1, :] * lane_sums(part, k), 0.0)


def outputs(alpha, beta, q0, q1, q2, q3, alpha_out, beta_out, mass_out):
    alpha_out[...] = alpha[...]
    beta_out[...] = beta[...]
    mass_out[...] = (q0[...] + q1[...]) + (q2[...] + q3[...])


def in_hbm(array):
    return pltpu.with_memory_space_constraint(array, pltpu.HBM)


def swapped(value, axis):
    return lax.ppermute(value, axis, [(0, 1), (1, 0)])


def across(value, k):
    return lax.ppermute(value, ROW_AXES, [(d, d ^ k) for d in range(4)])


def back(value, k):
    moves = [(z * 4 + g, (z ^ k) * 4 + g - 1) for z in range(2) for g in range(1, 4)]
    return lax.ppermute(value, ("z", "g"), moves)


def exchanged(copies):
    return lax.all_to_all(copies, COLUMN_AXES, split_axis=0, concat_axis=0, tiled=True)


def local(features, last_features, growth, cell_counts):
    part = pltpu.VMEM((ROWS, CELLS), F32)
    limits = pltpu.VMEM((COLUMN_BLOCKS, CELLS), F32)
    some_cells = shape(CELLS, WIDTH, dtype=BF16)
    row_parts = shape(8, CELLS)
    column_parts = shape(COLUMN_BLOCKS, COLUMN_BLOCKS, CELLS)

    with jax.named_scope("moments"):
        copies, own, last, frame = call(
            local_sums,
            (shape(COLUMN_BLOCKS, 8, CELLS), some_cells, some_cells, shape(FRAME, CELLS)),
            4,
            (
                pltpu.VMEM((1, CELLS, WIDTH), BF16),
                pltpu.VMEM((CELLS, WIDTH), BF16),
                pltpu.VMEM((1, CELLS), F32),
                pltpu.SMEM((5,), jnp.int32),
                pltpu.SemaphoreType.DMA((4,)),
            ),
            space=pltpu.HBM,
            name="local_sums",
        )(*(in_hbm(a) for a in (features, last_features, growth, cell_counts)))
        other = swapped(own, "c")
        messages = exchanged(copies)
    with jax.named_scope("gather"):
        targets = call(parcel, shape(COLUMN_BLOCKS, CELLS, WIDTH, dtype=BF16), 3, name="parcel")(
            frame, back(own, 0), last
        )
        anywhere = pl.BlockSpec(memory_space=pl.ANY)
        vmem = pl.BlockSpec(memory_space=pltpu.VMEM)
        sums, near, targets = pl.pallas_call(
            group_sums,
            out_shape=(
                row_parts,
                shape(2 * CELLS, WIDTH, dtype=BF16),
                shape(COLUMN_BLOCKS, CELLS, WIDTH, dtype=BF16),
            ),
            in_specs=[vmem] * 3 + [anywhere],
            out_specs=(vmem, vmem, anywhere),
            input_output_aliases={3: 2},
            compiler_params=pltpu.CompilerParams(vmem_limit_bytes=16 * 1024 * 1024),
            name="group_sums",
        )(messages, own, other, targets)
        targets = exchanged(targets)
        mine = call(core_sums, row_parts, 2, name="core_sums")(sums, swapped(sums, "c"))
        sums = (mine, swapped(mine, "z"), back(mine, 0), back(mine, 1))
        ready = call(
            prepared,
            (shape(ROWS, WIDTH, dtype=BF16), shape(ROWS, CELLS), row_parts),
            7,
            name="prepared",
        )(frame, *sums, near, swapped(near, "z"))

    def row_exchange(sums):
        return [sums] + [across(sums, k) for k in range(1, ROW_BLOCKS)]

    with jax.named_scope("first_rows"):
        scores, sums = call(
            first_pass,
            (shape(COLUMN_BLOCKS, ROWS, CELLS), row_parts),
            5,
            (part, limits),
            name="first_pass",
        )(frame, targets, *ready)
    with jax.named_scope("first_columns"):
        log_p, copies = call(
            first_columns,
            (shape(ROW_BLOCKS, CELLS), column_parts),
            6,
            (part, limits),
            name="first_columns",
        )(frame, *row_exchange(sums), scores)
        parts = exchanged(copies)
    with jax.named_scope("second_rows"):
        sums = call(second_rows, shape(ROW_BLOCKS, CELLS), 3, (part, limits), name="second_rows")(
            frame, parts, scores
        )
    with jax.named_scope("last_columns"):
        weights, source_pot, copies = call(
            last_columns,
            (shape(ROW_BLOCKS, CELLS), shape(1, CELLS), column_parts),
            7,
            (part, limits),
            name="last_columns",
        )(frame, log_p, *row_exchange(sums), scores)
        parts = exchanged(copies)
    with jax.named_scope("mass"):
        target_pot, *masses = call(
            last_rows, (shape(1, CELLS),) * 5, 4, (part, limits, limits), name="last_rows"
        )(frame, parts, scores, weights)
        masses = [masses[0]] + [across(masses[k], k) for k in range(1, ROW_BLOCKS)]
        return call(outputs, (shape(1, CELLS),) * 3, 6, name="outputs")(
            source_pot, target_pot, *masses
        )


def solution(mesh):
    fine = Mesh(mesh.devices.reshape(SIZES), AXES)
    blk = ("x", "z", "y", "c")
    return jax.shard_map(
        local,
        mesh=fine,
        in_specs=(P("g", blk, None), P(blk, None), P("g", blk), P()),
        out_specs=(P("g", blk),) * 3,
        check_vma=False,
    )
```

```python
import math

import jax
import jax.numpy as jnp
from jax import lax
from jax.experimental import pallas as pl
from jax.experimental.pallas import tpu as pltpu
from jax.sharding import Mesh
from jax.sharding import PartitionSpec as P

AXES = ("x", "z", "y", "c", "g")
SIZES = (4, 2, 4, 2, 4)
ROW_AXES = ("z", "c")
COLUMN_AXES = ("x", "y")

EPSILON = 0.1
PENALTY = 1.0
TAU = PENALTY / (PENALTY + EPSILON)
LOG2E = math.log2(math.e)
ABSENT = -1e30

CELLS = 128
WIDTH = 256
ROW_BLOCKS = 4
COLUMN_BLOCKS = 16
ROWS = ROW_BLOCKS * CELLS
STRIP = 64

COLUMNS_AT = 0
ROWS_AT = 16
N_S = 20
N_T = 21
GROWTH = 22
LAST_GROUP = 23
FRAME = 24

F32 = jnp.float32
BF16 = jnp.bfloat16


def shape(*dims, dtype=F32):
    return jax.ShapeDtypeStruct(dims, dtype)


def call(kernel, out_shape, n_inputs, scratch=(), space=pltpu.VMEM, awaited=0, name=None):
    return pl.pallas_call(
        kernel,
        out_shape=out_shape,
        in_specs=[pl.BlockSpec(memory_space=space)] * n_inputs
        + [pl.BlockSpec(memory_space=pl.ANY)] * awaited,
        out_specs=jax.tree.map(lambda _: pl.BlockSpec(memory_space=pltpu.VMEM), out_shape),
        scratch_shapes=list(scratch),
        compiler_params=pltpu.CompilerParams(vmem_limit_bytes=16 * 1024 * 1024),
        name=name,
    )


def block_start(x, z, y, c):
    return (((x * 2 + z) * 4 + y) * 2 + c) * CELLS


def own_sums(cells, present):
    kept = jnp.where(present, cells, 0.0)
    total = jnp.sum(kept, axis=0, keepdims=True)
    squares = jnp.sum(kept * kept, axis=0, keepdims=True)
    norm = jnp.sum(squares, axis=1, keepdims=True)
    zeros = jnp.zeros((1, CELLS), F32)
    return total[:, :CELLS], total[:, CELLS:], jnp.broadcast_to(norm, (1, CELLS)), zeros


def local_sums(
    features, last, growth, counts, copies, own_out, last_out, frame, own, final, rates, numbers, sems
):
    loads = [
        pltpu.make_async_copy(source, target, sems.at[i])
        for i, (source, target) in enumerate(
            ((features, own), (last, final), (growth, rates), (counts, numbers))
        )
    ]
    for load in loads:
        load.start()
    x, z, y, c, g = (lax.axis_index(a) for a in AXES)
    start = block_start(x, z, y, c)
    for load in reversed(loads):
        load.wait()
    count_source = numbers[g]
    count_target = numbers[g + 1]
    row = start + lax.broadcasted_iota(jnp.int32, (CELLS, 1), 0)
    rows = own_sums(own[0].astype(F32), row < count_source)
    rows += own_sums(final[...].astype(F32), row < numbers[4])
    copies[...] = jnp.broadcast_to(jnp.concatenate(rows, axis=0)[None], copies.shape)
    own_out[...] = own[0]
    last_out[...] = final[...]
    block = lax.broadcasted_iota(jnp.int32, (COLUMN_BLOCKS, CELLS), 0)
    lane = lax.broadcasted_iota(jnp.int32, (COLUMN_BLOCKS, CELLS), 1)
    target = block_start(block >> 2, z, block & 3, c) + lane
    frame[COLUMNS_AT : COLUMNS_AT + COLUMN_BLOCKS, :] = jnp.where(target < count_target, 1.0, 0.0)
    for k in range(ROW_BLOCKS):
        place = (z * 2 + c) ^ k
        source = block_start(x, place >> 1, y, place & 1) + lane[:1]
        frame[ROWS_AT + k : ROWS_AT + k + 1, :] = jnp.where(source < count_source, 1.0, 0.0)
    ones = jnp.ones((1, CELLS), F32)
    frame[N_S : N_S + 1, :] = ones * count_source.astype(F32)
    frame[N_T : N_T + 1, :] = ones * count_target.astype(F32)
    frame[GROWTH : GROWTH + 1, :] = rates[...]
    frame[LAST_GROUP : LAST_GROUP + 1, :] = ones * (g == 3).astype(F32)


def parcel(frame, shifted, last, copies):
    is_last = frame[LAST_GROUP : LAST_GROUP + 1, :] > 0.0
    wide_last = jnp.concatenate([is_last, is_last], axis=1)
    targets = jnp.where(wide_last, last[...].astype(F32), shifted[...].astype(F32)).astype(BF16)
    for i in range(COLUMN_BLOCKS):
        copies[i] = targets


def group_sums(messages, own, copies, sums, own_out, copies_out):
    sums[...] = jnp.sum(messages[...], axis=0)
    own_out[...] = own[...]


def core_sums(mine, other, own, other_own, out, near):
    out[...] = mine[...] + other[...]
    near[:CELLS, :] = own[...]
    near[CELLS:, :] = other_own[...]


def prepared(frame, mine, across, back, back_across, near, far, rows, weights, scales):
    is_last = frame[LAST_GROUP : LAST_GROUP + 1, :] > 0.0
    sources = mine[...] + across[...]
    targets = jnp.where(is_last, sources[4:8], (back[...] + back_across[...])[0:4])
    n_s = frame[N_S : N_S + 1, :]
    n_t = frame[N_T : N_T + 1, :]
    products = (sources[0:2] / n_s) * (targets[0:2] / n_t)
    dot = jnp.sum(jnp.sum(products, axis=0, keepdims=True), axis=1, keepdims=True)
    spread = sources[2:3] / n_s + targets[2:3] / n_t - 2.0 * dot
    scale = LOG2E / (EPSILON * spread)
    scales[...] = jnp.broadcast_to(scale, scales.shape)
    for k, block in enumerate((near[...], far[...])):
        at = slice(k * 2 * CELLS, (k + 1) * 2 * CELLS)
        rows[at, :] = block
        wide = block.astype(F32)
        weights[at, :] = jnp.sum(wide * wide, axis=1, keepdims=True) * scale


def lane_sums(part, k):
    return jnp.sum(part[k * CELLS : (k + 1) * CELLS, :].T, axis=0, keepdims=True)


def first_pass(frame, targets, rows, weights, scales, scores, sums, part, limits):
    part[...] = jnp.zeros_like(part)
    limits[...] = jnp.where(frame[COLUMNS_AT : COLUMNS_AT + COLUMN_BLOCKS, :] > 0.0, 0.0, ABSENT)
    scale = scales[0:1, :]
    twice = 2.0 * scale

    @pl.loop(0, COLUMN_BLOCKS // 2)
    def _(pair):
        first = pair * 2
        block = targets[pl.ds(first, 2)].reshape(2 * CELLS, WIDTH)
        products = lax.dot_general(
            rows[...], block, (((1,), (1,)), ((), ())), preferred_element_type=F32
        )
        running = part[...]
        for half in range(2):
            wide = targets[first + half].astype(F32)
            squares = wide * wide
            norms = jnp.sum((squares[:, :CELLS] + squares[:, CELLS:]).T, axis=0, keepdims=True)
            tile = (weights[...] + norms * scale) - twice * products[
                :, half * CELLS : (half + 1) * CELLS
            ]
            scores[first + half] = tile
            running = running + jnp.exp2(limits[pl.ds(first + half, 1), :] - tile)
        part[...] = running

    for k in range(ROW_BLOCKS):
        sums[k : k + 1, :] = lane_sums(part, k)
    sums[4:5, :] = frame[GROWTH : GROWTH + 1, :]
    sums[5:8, :] = jnp.zeros((3, CELLS), F32)


def column_pass(frame, alpha, scores, out, spread_out, gathered):
    for k in range(ROW_BLOCKS):
        present = frame[ROWS_AT + k : ROWS_AT + k + 1, :] > 0.0
        limit = jnp.where(present, alpha[k] * LOG2E, ABSENT)
        spread_out[k * CELLS : (k + 1) * CELLS, :] = jnp.broadcast_to(limit, (CELLS, CELLS)).T

    def strip(number, running):
        at = pl.ds(pl.multiple_of(number * STRIP, STRIP), STRIP)
        limit = spread_out[at, :]
        more = []
        for i, total in enumerate(running):
            terms = jnp.exp2(limit - scores[i, at, :])
            more.append(total + jnp.sum(terms.reshape(STRIP // 8, 8, CELLS), axis=0))
        return tuple(more)

    zeros = (jnp.zeros((8, CELLS), F32),) * COLUMN_BLOCKS
    for i, total in enumerate(lax.fori_loop(0, ROWS // STRIP, strip, zeros)):
        gathered[i : i + 1, :] = jnp.sum(total, axis=0, keepdims=True)
    out[...] = jnp.broadcast_to(gathered[...][None], out.shape)


def new_alphas(frame, parts, log_p):
    alphas = []
    for k in range(ROW_BLOCKS):
        total = parts[0][k : k + 1, :]
        for j in range(1, ROW_BLOCKS):
            total = total + parts[j][(k ^ j) : (k ^ j) + 1, :]
        present = frame[ROWS_AT + k : ROWS_AT + k + 1, :] > 0.0
        alphas.append(jnp.where(present, TAU * (log_p[k] - jnp.log(total)), 0.0))
    return alphas


def first_columns(frame, p0, p1, p2, p3, scores, log_out, out, spread_out, gathered):
    n_s = frame[N_S : N_S + 1, :]
    parts = (p0, p1, p2, p3)
    log_p = [jnp.log(part[4:5, :] / n_s) for part in parts]
    for k in range(ROW_BLOCKS):
        log_out[k : k + 1, :] = log_p[k]
    column_pass(frame, new_alphas(frame, parts, log_p), scores, out, spread_out, gathered)


def last_columns(
    frame, log_p, p0, p1, p2, p3, scores, weights, alpha_out, out, spread_out, gathered
):
    n_s = frame[N_S : N_S + 1, :]
    log_rows = [log_p[k : k + 1, :] for k in range(ROW_BLOCKS)]
    alphas = new_alphas(frame, (p0, p1, p2, p3), log_rows)
    alpha_out[...] = alphas[0]
    for k in range(ROW_BLOCKS):
        present = frame[ROWS_AT + k : ROWS_AT + k + 1, :]
        weights[k : k + 1, :] = present * n_s * jnp.exp(alphas[k])
    column_pass(frame, alphas, scores, out, spread_out, gathered)


def row_pass(frame, parts, scores, part, limits):
    n_t = frame[N_T : N_T + 1, :]
    total = jnp.sum(parts[...], axis=0)
    beta = TAU * (-jnp.log(n_t) - jnp.log(total))
    present = frame[COLUMNS_AT : COLUMNS_AT + COLUMN_BLOCKS, :] > 0.0
    limits[...] = jnp.where(present, beta * LOG2E, ABSENT)

    @pl.loop(0, ROWS // STRIP)
    def _(number):
        at = pl.ds(pl.multiple_of(number * STRIP, STRIP), STRIP)
        running = jnp.exp2(limits[0:1, :] - scores[0, at, :])
        for i in range(1, COLUMN_BLOCKS):
            running = running + jnp.exp2(limits[i : i + 1, :] - scores[i, at, :])
        part[at, :] = running

    return jnp.where(present, beta, 0.0)


def second_rows(frame, parts, scores, sums, part, limits):
    row_pass(frame, parts, scores, part, limits)
    for k in range(ROW_BLOCKS):
        sums[k : k + 1, :] = lane_sums(part, k)


def last_rows(frame, parts, scores, weights, beta_out, q0, q1, q2, q3, part, limits, betas):
    betas[...] = row_pass(frame, parts, scores, part, limits)
    place = lax.axis_index("x") * 4 + lax.axis_index("y")
    beta_out[...] = betas[pl.ds(place, 1), :]
    for k, out in enumerate((q0, q1, q2, q3)):
        present = frame[ROWS_AT + k : ROWS_AT + k + 1, :] > 0.0
        out[...] = jnp.where(present, weights[k : k + 1, :] * lane_sums(part, k), 0.0)


def outputs(alpha, beta, q0, q1, q2, q3, alpha_out, beta_out, mass_out):
    alpha_out[...] = alpha[...]
    beta_out[...] = beta[...]
    mass_out[...] = (q0[...] + q1[...]) + (q2[...] + q3[...])


def in_hbm(array):
    return pltpu.with_memory_space_constraint(array, pltpu.HBM)


def swapped(value, axis):
    return lax.ppermute(value, axis, [(0, 1), (1, 0)])


def across(value, k):
    return lax.ppermute(value, ROW_AXES, [(d, d ^ k) for d in range(4)])


def back(value, k):
    moves = [(z * 4 + g, (z ^ k) * 4 + g - 1) for z in range(2) for g in range(1, 4)]
    return lax.ppermute(value, ("z", "g"), moves)


def exchanged(copies):
    return lax.all_to_all(copies, COLUMN_AXES, split_axis=0, concat_axis=0, tiled=True)


def local(features, last_features, growth, cell_counts):
    part = pltpu.VMEM((ROWS, CELLS), F32)
    limits = pltpu.VMEM((COLUMN_BLOCKS, CELLS), F32)
    some_cells = shape(CELLS, WIDTH, dtype=BF16)
    row_parts = shape(8, CELLS)
    column_parts = shape(COLUMN_BLOCKS, COLUMN_BLOCKS, CELLS)

    with jax.named_scope("moments"):
        copies, own, last, frame = call(
            local_sums,
            (shape(COLUMN_BLOCKS, 8, CELLS), some_cells, some_cells, shape(FRAME, CELLS)),
            4,
            (
                pltpu.VMEM((1, CELLS, WIDTH), BF16),
                pltpu.VMEM((CELLS, WIDTH), BF16),
                pltpu.VMEM((1, CELLS), F32),
                pltpu.SMEM((5,), jnp.int32),
                pltpu.SemaphoreType.DMA((4,)),
            ),
            space=pltpu.HBM,
            name="local_sums",
        )(*(in_hbm(a) for a in (features, last_features, growth, cell_counts)))
        messages = exchanged(copies)
    with jax.named_scope("gather"):
        targets = call(parcel, shape(COLUMN_BLOCKS, CELLS, WIDTH, dtype=BF16), 3, name="parcel")(
            frame, back(own, 0), last
        )
        anywhere = pl.BlockSpec(memory_space=pl.ANY)
        vmem = pl.BlockSpec(memory_space=pltpu.VMEM)
        sums, own, targets = pl.pallas_call(
            group_sums,
            out_shape=(
                row_parts,
                some_cells,
                shape(COLUMN_BLOCKS, CELLS, WIDTH, dtype=BF16),
            ),
            in_specs=[vmem] * 2 + [anywhere],
            out_specs=(vmem, vmem, anywhere),
            input_output_aliases={2: 2},
            compiler_params=pltpu.CompilerParams(vmem_limit_bytes=16 * 1024 * 1024),
            name="group_sums",
        )(messages, own, targets)
        targets = exchanged(targets)
        sums, near = call(
            core_sums, (row_parts, shape(2 * CELLS, WIDTH, dtype=BF16)), 4, name="core_sums"
        )(sums, swapped(sums, "c"), own, swapped(own, "c"))
        sums = (sums, swapped(sums, "z"), back(sums, 0), back(sums, 1))
        ready = call(
            prepared,
            (shape(ROWS, WIDTH, dtype=BF16), shape(ROWS, CELLS), row_parts),
            7,
            name="prepared",
        )(frame, *sums, near, swapped(near, "z"))

    def row_exchange(sums):
        return [sums] + [across(sums, k) for k in range(1, ROW_BLOCKS)]

    with jax.named_scope("first_rows"):
        scores, sums = call(
            first_pass,
            (shape(COLUMN_BLOCKS, ROWS, CELLS), row_parts),
            5,
            (part, limits),
            name="first_pass",
        )(frame, targets, *ready)
    with jax.named_scope("first_columns"):
        log_p, copies = call(
            first_columns,
            (shape(ROW_BLOCKS, CELLS), column_parts),
            6,
            (part, limits),
            name="first_columns",
        )(frame, *row_exchange(sums), scores)
        parts = exchanged(copies)
    with jax.named_scope("second_rows"):
        sums = call(second_rows, shape(ROW_BLOCKS, CELLS), 3, (part, limits), name="second_rows")(
            frame, parts, scores
        )
    with jax.named_scope("last_columns"):
        weights, source_pot, copies = call(
            last_columns,
            (shape(ROW_BLOCKS, CELLS), shape(1, CELLS), column_parts),
            7,
            (part, limits),
            name="last_columns",
        )(frame, log_p, *row_exchange(sums), scores)
        parts = exchanged(copies)
    with jax.named_scope("mass"):
        target_pot, *masses = call(
            last_rows, (shape(1, CELLS),) * 5, 4, (part, limits, limits), name="last_rows"
        )(frame, parts, scores, weights)
        masses = [masses[0]] + [across(masses[k], k) for k in range(1, ROW_BLOCKS)]
        return call(outputs, (shape(1, CELLS),) * 3, 6, name="outputs")(
            source_pot, target_pot, *masses
        )


def solution(mesh):
    fine = Mesh(mesh.devices.reshape(SIZES), AXES)
    blk = ("x", "z", "y", "c")
    return jax.shard_map(
        local,
        mesh=fine,
        in_specs=(P("g", blk, None), P(blk, None), P("g", blk), P()),
        out_specs=(P("g", blk),) * 3,
        check_vma=False,
    )
```

```python
import math

import jax
import jax.numpy as jnp
from jax import lax
from jax.experimental import pallas as pl
from jax.experimental.pallas import tpu as pltpu
from jax.sharding import Mesh
from jax.sharding import PartitionSpec as P

AXES = ("x", "z", "y", "c", "g")
SIZES = (4, 2, 4, 2, 4)
ROW_AXES = ("z", "c")
COLUMN_AXES = ("x", "y")

EPSILON = 0.1
PENALTY = 1.0
TAU = PENALTY / (PENALTY + EPSILON)
LOG2E = math.log2(math.e)
ABSENT = -1e30

CELLS = 128
WIDTH = 256
ROW_BLOCKS = 4
COLUMN_BLOCKS = 16
ROWS = ROW_BLOCKS * CELLS
STRIP = 64

COLUMNS_AT = 0
ROWS_AT = 16
N_S = 20
N_T = 21
GROWTH = 22
LAST_GROUP = 23
FRAME = 24

F32 = jnp.float32
BF16 = jnp.bfloat16


def shape(*dims, dtype=F32):
    return jax.ShapeDtypeStruct(dims, dtype)


def call(kernel, out_shape, n_inputs, scratch=(), space=pltpu.VMEM, awaited=0, name=None):
    return pl.pallas_call(
        kernel,
        out_shape=out_shape,
        in_specs=[pl.BlockSpec(memory_space=space)] * n_inputs
        + [pl.BlockSpec(memory_space=pl.ANY)] * awaited,
        out_specs=jax.tree.map(lambda _: pl.BlockSpec(memory_space=pltpu.VMEM), out_shape),
        scratch_shapes=list(scratch),
        compiler_params=pltpu.CompilerParams(vmem_limit_bytes=16 * 1024 * 1024),
        name=name,
    )


def block_start(x, z, y, c):
    return (((x * 2 + z) * 4 + y) * 2 + c) * CELLS


def own_sums(cells, present):
    kept = jnp.where(present, cells, 0.0)
    total = jnp.sum(kept, axis=0, keepdims=True)
    squares = jnp.sum(kept * kept, axis=0, keepdims=True)
    norm = jnp.sum(squares, axis=1, keepdims=True)
    zeros = jnp.zeros((1, CELLS), F32)
    return total[:, :CELLS], total[:, CELLS:], jnp.broadcast_to(norm, (1, CELLS)), zeros


def local_sums(
    features, last, growth, counts, copies, own_out, last_out, frame, own, final, rates, numbers, sems
):
    loads = [
        pltpu.make_async_copy(source, target, sems.at[i])
        for i, (source, target) in enumerate(
            ((features, own), (last, final), (growth, rates), (counts, numbers))
        )
    ]
    for load in loads:
        load.start()
    x, z, y, c, g = (lax.axis_index(a) for a in AXES)
    start = block_start(x, z, y, c)
    for load in reversed(loads):
        load.wait()
    count_source = numbers[g]
    count_target = numbers[g + 1]
    row = start + lax.broadcasted_iota(jnp.int32, (CELLS, 1), 0)
    rows = own_sums(own[0].astype(F32), row < count_source)
    rows += own_sums(final[...].astype(F32), row < numbers[4])
    copies[...] = jnp.broadcast_to(jnp.concatenate(rows, axis=0)[None], copies.shape)
    own_out[...] = own[0]
    last_out[...] = final[...]
    block = lax.broadcasted_iota(jnp.int32, (COLUMN_BLOCKS, CELLS), 0)
    lane = lax.broadcasted_iota(jnp.int32, (COLUMN_BLOCKS, CELLS), 1)
    target = block_start(block >> 2, z, block & 3, c) + lane
    frame[COLUMNS_AT : COLUMNS_AT + COLUMN_BLOCKS, :] = jnp.where(target < count_target, 1.0, 0.0)
    for k in range(ROW_BLOCKS):
        place = (z * 2 + c) ^ k
        source = block_start(x, place >> 1, y, place & 1) + lane[:1]
        frame[ROWS_AT + k : ROWS_AT + k + 1, :] = jnp.where(source < count_source, 1.0, 0.0)
    ones = jnp.ones((1, CELLS), F32)
    frame[N_S : N_S + 1, :] = ones * count_source.astype(F32)
    frame[N_T : N_T + 1, :] = ones * count_target.astype(F32)
    frame[GROWTH : GROWTH + 1, :] = rates[...]
    frame[LAST_GROUP : LAST_GROUP + 1, :] = ones * (g == 3).astype(F32)


def parcel(frame, shifted, last, copies):
    is_last = frame[LAST_GROUP : LAST_GROUP + 1, :] > 0.0
    wide_last = jnp.concatenate([is_last, is_last], axis=1)
    targets = jnp.where(wide_last, last[...].astype(F32), shifted[...].astype(F32)).astype(BF16)
    for i in range(COLUMN_BLOCKS):
        copies[i] = targets


def group_sums(messages, own, copies, sums, own_out, copies_out):
    sums[...] = jnp.sum(messages[...], axis=0)
    own_out[...] = own[...]


def core_sums(mine, other, own, other_own, out, near):
    out[...] = mine[...] + other[...]
    near[:CELLS, :] = own[...]
    near[CELLS:, :] = other_own[...]


def prepared(frame, mine, across, back, back_across, near, far, rows, weights, scales):
    is_last = frame[LAST_GROUP : LAST_GROUP + 1, :] > 0.0
    sources = mine[...] + across[...]
    targets = jnp.where(is_last, sources[4:8], (back[...] + back_across[...])[0:4])
    n_s = frame[N_S : N_S + 1, :]
    n_t = frame[N_T : N_T + 1, :]
    products = (sources[0:2] / n_s) * (targets[0:2] / n_t)
    dot = jnp.sum(jnp.sum(products, axis=0, keepdims=True), axis=1, keepdims=True)
    spread = sources[2:3] / n_s + targets[2:3] / n_t - 2.0 * dot
    scale = LOG2E / (EPSILON * spread)
    scales[...] = jnp.broadcast_to(scale, scales.shape)
    for k, block in enumerate((near[...], far[...])):
        at = slice(k * 2 * CELLS, (k + 1) * 2 * CELLS)
        rows[at, :] = block
        wide = block.astype(F32)
        weights[at, :] = jnp.sum(wide * wide, axis=1, keepdims=True) * scale


def lane_sums(part, k):
    return jnp.sum(part[k * CELLS : (k + 1) * CELLS, :].T, axis=0, keepdims=True)


def first_pass(frame, targets, rows, weights, scales, scores, sums, part, limits):
    part[...] = jnp.zeros_like(part)
    limits[...] = jnp.where(frame[COLUMNS_AT : COLUMNS_AT + COLUMN_BLOCKS, :] > 0.0, 0.0, ABSENT)
    scale = scales[0:1, :]
    twice = 2.0 * scale

    @pl.loop(0, COLUMN_BLOCKS // 2, unroll=8)
    def _(pair):
        first = pair * 2
        block = targets[pl.ds(first, 2)].reshape(2 * CELLS, WIDTH)
        products = lax.dot_general(
            rows[...], block, (((1,), (1,)), ((), ())), preferred_element_type=F32
        )
        running = part[...]
        for half in range(2):
            wide = targets[first + half].astype(F32)
            squares = wide * wide
            norms = jnp.sum((squares[:, :CELLS] + squares[:, CELLS:]).T, axis=0, keepdims=True)
            tile = (weights[...] + norms * scale) - twice * products[
                :, half * CELLS : (half + 1) * CELLS
            ]
            scores[first + half] = tile
            running = running + jnp.exp2(limits[pl.ds(first + half, 1), :] - tile)
        part[...] = running

    for k in range(ROW_BLOCKS):
        sums[k : k + 1, :] = lane_sums(part, k)
    sums[4:5, :] = frame[GROWTH : GROWTH + 1, :]
    sums[5:8, :] = jnp.zeros((3, CELLS), F32)


def column_pass(frame, alpha, scores, out, spread_out, gathered):
    for k in range(ROW_BLOCKS):
        present = frame[ROWS_AT + k : ROWS_AT + k + 1, :] > 0.0
        limit = jnp.where(present, alpha[k] * LOG2E, ABSENT)
        spread_out[k * CELLS : (k + 1) * CELLS, :] = jnp.broadcast_to(limit, (CELLS, CELLS)).T

    def strip(number, running):
        at = pl.ds(pl.multiple_of(number * STRIP, STRIP), STRIP)
        limit = spread_out[at, :]
        more = []
        for i, total in enumerate(running):
            terms = jnp.exp2(limit - scores[i, at, :])
            more.append(total + jnp.sum(terms.reshape(STRIP // 8, 8, CELLS), axis=0))
        return tuple(more)

    zeros = (jnp.zeros((8, CELLS), F32),) * COLUMN_BLOCKS
    for i, total in enumerate(lax.fori_loop(0, ROWS // STRIP, strip, zeros, unroll=8)):
        gathered[i : i + 1, :] = jnp.sum(total, axis=0, keepdims=True)
    out[...] = jnp.broadcast_to(gathered[...][None], out.shape)


def new_alphas(frame, parts, log_p):
    alphas = []
    for k in range(ROW_BLOCKS):
        total = parts[0][k : k + 1, :]
        for j in range(1, ROW_BLOCKS):
            total = total + parts[j][(k ^ j) : (k ^ j) + 1, :]
        present = frame[ROWS_AT + k : ROWS_AT + k + 1, :] > 0.0
        alphas.append(jnp.where(present, TAU * (log_p[k] - jnp.log(total)), 0.0))
    return alphas


def first_columns(frame, p0, p1, p2, p3, scores, log_out, out, spread_out, gathered):
    n_s = frame[N_S : N_S + 1, :]
    parts = (p0, p1, p2, p3)
    log_p = [jnp.log(part[4:5, :] / n_s) for part in parts]
    for k in range(ROW_BLOCKS):
        log_out[k : k + 1, :] = log_p[k]
    column_pass(frame, new_alphas(frame, parts, log_p), scores, out, spread_out, gathered)


def last_columns(
    frame, log_p, p0, p1, p2, p3, scores, weights, alpha_out, out, spread_out, gathered
):
    n_s = frame[N_S : N_S + 1, :]
    log_rows = [log_p[k : k + 1, :] for k in range(ROW_BLOCKS)]
    alphas = new_alphas(frame, (p0, p1, p2, p3), log_rows)
    alpha_out[...] = alphas[0]
    for k in range(ROW_BLOCKS):
        present = frame[ROWS_AT + k : ROWS_AT + k + 1, :]
        weights[k : k + 1, :] = present * n_s * jnp.exp(alphas[k])
    column_pass(frame, alphas, scores, out, spread_out, gathered)


def row_pass(frame, parts, scores, part, limits):
    n_t = frame[N_T : N_T + 1, :]
    total = jnp.sum(parts[...], axis=0)
    beta = TAU * (-jnp.log(n_t) - jnp.log(total))
    present = frame[COLUMNS_AT : COLUMNS_AT + COLUMN_BLOCKS, :] > 0.0
    limits[...] = jnp.where(present, beta * LOG2E, ABSENT)

    @pl.loop(0, ROWS // STRIP, unroll=8)
    def _(number):
        at = pl.ds(pl.multiple_of(number * STRIP, STRIP), STRIP)
        running = jnp.exp2(limits[0:1, :] - scores[0, at, :])
        for i in range(1, COLUMN_BLOCKS):
            running = running + jnp.exp2(limits[i : i + 1, :] - scores[i, at, :])
        part[at, :] = running

    return jnp.where(present, beta, 0.0)


def second_rows(frame, parts, scores, sums, part, limits):
    row_pass(frame, parts, scores, part, limits)
    for k in range(ROW_BLOCKS):
        sums[k : k + 1, :] = lane_sums(part, k)


def last_rows(frame, parts, scores, weights, beta_out, q0, q1, q2, q3, part, limits, betas):
    betas[...] = row_pass(frame, parts, scores, part, limits)
    place = lax.axis_index("x") * 4 + lax.axis_index("y")
    beta_out[...] = betas[pl.ds(place, 1), :]
    for k, out in enumerate((q0, q1, q2, q3)):
        present = frame[ROWS_AT + k : ROWS_AT + k + 1, :] > 0.0
        out[...] = jnp.where(present, weights[k : k + 1, :] * lane_sums(part, k), 0.0)


def outputs(alpha, beta, q0, q1, q2, q3, alpha_out, beta_out, mass_out):
    alpha_out[...] = alpha[...]
    beta_out[...] = beta[...]
    mass_out[...] = (q0[...] + q1[...]) + (q2[...] + q3[...])


def in_hbm(array):
    return pltpu.with_memory_space_constraint(array, pltpu.HBM)


def swapped(value, axis):
    return lax.ppermute(value, axis, [(0, 1), (1, 0)])


def across(value, k):
    return lax.ppermute(value, ROW_AXES, [(d, d ^ k) for d in range(4)])


def back(value, k):
    moves = [(z * 4 + g, (z ^ k) * 4 + g - 1) for z in range(2) for g in range(1, 4)]
    return lax.ppermute(value, ("z", "g"), moves)


def exchanged(copies):
    return lax.all_to_all(copies, COLUMN_AXES, split_axis=0, concat_axis=0, tiled=True)


def local(features, last_features, growth, cell_counts):
    part = pltpu.VMEM((ROWS, CELLS), F32)
    limits = pltpu.VMEM((COLUMN_BLOCKS, CELLS), F32)
    some_cells = shape(CELLS, WIDTH, dtype=BF16)
    row_parts = shape(8, CELLS)
    column_parts = shape(COLUMN_BLOCKS, COLUMN_BLOCKS, CELLS)

    with jax.named_scope("moments"):
        copies, own, last, frame = call(
            local_sums,
            (shape(COLUMN_BLOCKS, 8, CELLS), some_cells, some_cells, shape(FRAME, CELLS)),
            4,
            (
                pltpu.VMEM((1, CELLS, WIDTH), BF16),
                pltpu.VMEM((CELLS, WIDTH), BF16),
                pltpu.VMEM((1, CELLS), F32),
                pltpu.SMEM((5,), jnp.int32),
                pltpu.SemaphoreType.DMA((4,)),
            ),
            space=pltpu.HBM,
            name="local_sums",
        )(*(in_hbm(a) for a in (features, last_features, growth, cell_counts)))
        messages = exchanged(copies)
    with jax.named_scope("gather"):
        targets = call(parcel, shape(COLUMN_BLOCKS, CELLS, WIDTH, dtype=BF16), 3, name="parcel")(
            frame, back(own, 0), last
        )
        anywhere = pl.BlockSpec(memory_space=pl.ANY)
        vmem = pl.BlockSpec(memory_space=pltpu.VMEM)
        sums, own, targets = pl.pallas_call(
            group_sums,
            out_shape=(
                row_parts,
                some_cells,
                shape(COLUMN_BLOCKS, CELLS, WIDTH, dtype=BF16),
            ),
            in_specs=[vmem] * 2 + [anywhere],
            out_specs=(vmem, vmem, anywhere),
            input_output_aliases={2: 2},
            compiler_params=pltpu.CompilerParams(vmem_limit_bytes=16 * 1024 * 1024),
            name="group_sums",
        )(messages, own, targets)
        targets = exchanged(targets)
        sums, near = call(
            core_sums, (row_parts, shape(2 * CELLS, WIDTH, dtype=BF16)), 4, name="core_sums"
        )(sums, swapped(sums, "c"), own, swapped(own, "c"))
        sums = (sums, swapped(sums, "z"), back(sums, 0), back(sums, 1))
        ready = call(
            prepared,
            (shape(ROWS, WIDTH, dtype=BF16), shape(ROWS, CELLS), row_parts),
            7,
            name="prepared",
        )(frame, *sums, near, swapped(near, "z"))

    def row_exchange(sums):
        return [sums] + [across(sums, k) for k in range(1, ROW_BLOCKS)]

    with jax.named_scope("first_rows"):
        scores, sums = call(
            first_pass,
            (shape(COLUMN_BLOCKS, ROWS, CELLS), row_parts),
            5,
            (part, limits),
            name="first_pass",
        )(frame, targets, *ready)
    with jax.named_scope("first_columns"):
        log_p, copies = call(
            first_columns,
            (shape(ROW_BLOCKS, CELLS), column_parts),
            6,
            (part, limits),
            name="first_columns",
        )(frame, *row_exchange(sums), scores)
        parts = exchanged(copies)
    with jax.named_scope("second_rows"):
        sums = call(second_rows, shape(ROW_BLOCKS, CELLS), 3, (part, limits), name="second_rows")(
            frame, parts, scores
        )
    with jax.named_scope("last_columns"):
        weights, source_pot, copies = call(
            last_columns,
            (shape(ROW_BLOCKS, CELLS), shape(1, CELLS), column_parts),
            7,
            (part, limits),
            name="last_columns",
        )(frame, log_p, *row_exchange(sums), scores)
        parts = exchanged(copies)
    with jax.named_scope("mass"):
        target_pot, *masses = call(
            last_rows, (shape(1, CELLS),) * 5, 4, (part, limits, limits), name="last_rows"
        )(frame, parts, scores, weights)
        masses = [masses[0]] + [across(masses[k], k) for k in range(1, ROW_BLOCKS)]
        return call(outputs, (shape(1, CELLS),) * 3, 6, name="outputs")(
            source_pot, target_pot, *masses
        )


def solution(mesh):
    fine = Mesh(mesh.devices.reshape(SIZES), AXES)
    blk = ("x", "z", "y", "c")
    return jax.shard_map(
        local,
        mesh=fine,
        in_specs=(P("g", blk, None), P(blk, None), P("g", blk), P()),
        out_specs=(P("g", blk),) * 3,
        check_vma=False,
    )
```

```python
import math

import jax
import jax.numpy as jnp
from jax import lax
from jax.experimental import pallas as pl
from jax.experimental.pallas import tpu as pltpu
from jax.sharding import Mesh
from jax.sharding import PartitionSpec as P

AXES = ("x", "z", "y", "c", "g")
SIZES = (4, 2, 4, 2, 4)
ROW_AXES = ("z", "c")
COLUMN_AXES = ("x", "y")

EPSILON = 0.1
PENALTY = 1.0
TAU = PENALTY / (PENALTY + EPSILON)
LOG2E = math.log2(math.e)
ABSENT = -1e30

CELLS = 128
WIDTH = 256
ROW_BLOCKS = 4
COLUMN_BLOCKS = 16
ROWS = ROW_BLOCKS * CELLS
STRIP = 64

COLUMNS_AT = 0
ROWS_AT = 16
N_S = 20
N_T = 21
GROWTH = 22
LAST_GROUP = 23
FRAME = 24

F32 = jnp.float32
BF16 = jnp.bfloat16


def shape(*dims, dtype=F32):
    return jax.ShapeDtypeStruct(dims, dtype)


def call(kernel, out_shape, n_inputs, scratch=(), space=pltpu.VMEM, awaited=0, name=None):
    return pl.pallas_call(
        kernel,
        out_shape=out_shape,
        in_specs=[pl.BlockSpec(memory_space=space)] * n_inputs
        + [pl.BlockSpec(memory_space=pl.ANY)] * awaited,
        out_specs=jax.tree.map(lambda _: pl.BlockSpec(memory_space=pltpu.VMEM), out_shape),
        scratch_shapes=list(scratch),
        compiler_params=pltpu.CompilerParams(vmem_limit_bytes=16 * 1024 * 1024),
        name=name,
    )


def block_start(x, z, y, c):
    return (((x * 2 + z) * 4 + y) * 2 + c) * CELLS


def own_sums(cells, present):
    kept = jnp.where(present, cells, 0.0)
    total = jnp.sum(kept, axis=0, keepdims=True)
    squares = jnp.sum(kept * kept, axis=0, keepdims=True)
    norm = jnp.sum(squares, axis=1, keepdims=True)
    zeros = jnp.zeros((1, CELLS), F32)
    return total[:, :CELLS], total[:, CELLS:], jnp.broadcast_to(norm, (1, CELLS)), zeros


def local_sums(
    features, last, growth, counts, copies, own_out, last_out, frame, own, final, rates, numbers, sems
):
    loads = [
        pltpu.make_async_copy(source, target, sems.at[i])
        for i, (source, target) in enumerate(
            ((features, own), (last, final), (growth, rates), (counts, numbers))
        )
    ]
    for load in loads:
        load.start()
    x, z, y, c, g = (lax.axis_index(a) for a in AXES)
    start = block_start(x, z, y, c)
    for load in reversed(loads):
        load.wait()
    count_source = numbers[g]
    count_target = numbers[g + 1]
    row = start + lax.broadcasted_iota(jnp.int32, (CELLS, 1), 0)
    rows = own_sums(own[0].astype(F32), row < count_source)
    rows += own_sums(final[...].astype(F32), row < numbers[4])
    copies[...] = jnp.broadcast_to(jnp.concatenate(rows, axis=0)[None], copies.shape)
    own_out[...] = own[0]
    last_out[...] = final[...]
    block = lax.broadcasted_iota(jnp.int32, (COLUMN_BLOCKS, CELLS), 0)
    lane = lax.broadcasted_iota(jnp.int32, (COLUMN_BLOCKS, CELLS), 1)
    target = block_start(block >> 2, z, block & 3, c) + lane
    frame[COLUMNS_AT : COLUMNS_AT + COLUMN_BLOCKS, :] = jnp.where(target < count_target, 1.0, 0.0)
    for k in range(ROW_BLOCKS):
        place = (z * 2 + c) ^ k
        source = block_start(x, place >> 1, y, place & 1) + lane[:1]
        frame[ROWS_AT + k : ROWS_AT + k + 1, :] = jnp.where(source < count_source, 1.0, 0.0)
    ones = jnp.ones((1, CELLS), F32)
    frame[N_S : N_S + 1, :] = ones * count_source.astype(F32)
    frame[N_T : N_T + 1, :] = ones * count_target.astype(F32)
    frame[GROWTH : GROWTH + 1, :] = rates[...]
    frame[LAST_GROUP : LAST_GROUP + 1, :] = ones * (g == 3).astype(F32)


def parcel(frame, shifted, last, copies):
    is_last = frame[LAST_GROUP : LAST_GROUP + 1, :] > 0.0
    wide_last = jnp.concatenate([is_last, is_last], axis=1)
    targets = jnp.where(wide_last, last[...].astype(F32), shifted[...].astype(F32)).astype(BF16)
    for i in range(COLUMN_BLOCKS):
        copies[i] = targets


def group_sums(messages, own, copies, sums, own_out, copies_out):
    sums[...] = jnp.sum(messages[...], axis=0)
    own_out[...] = own[...]


def core_sums(mine, other, own, other_own, out, near):
    out[...] = mine[...] + other[...]
    near[:CELLS, :] = own[...]
    near[CELLS:, :] = other_own[...]


def prepared(frame, mine, across, back, back_across, near, far, rows, weights, scales):
    is_last = frame[LAST_GROUP : LAST_GROUP + 1, :] > 0.0
    sources = mine[...] + across[...]
    targets = jnp.where(is_last, sources[4:8], (back[...] + back_across[...])[0:4])
    n_s = frame[N_S : N_S + 1, :]
    n_t = frame[N_T : N_T + 1, :]
    products = (sources[0:2] / n_s) * (targets[0:2] / n_t)
    dot = jnp.sum(jnp.sum(products, axis=0, keepdims=True), axis=1, keepdims=True)
    spread = sources[2:3] / n_s + targets[2:3] / n_t - 2.0 * dot
    scale = LOG2E / (EPSILON * spread)
    scales[...] = jnp.broadcast_to(scale, scales.shape)
    for k, block in enumerate((near[...], far[...])):
        at = slice(k * 2 * CELLS, (k + 1) * 2 * CELLS)
        rows[at, :] = block
        wide = block.astype(F32)
        weights[at, :] = jnp.sum(wide * wide, axis=1, keepdims=True) * scale


def lane_sums(part, k):
    return jnp.sum(part[k * CELLS : (k + 1) * CELLS, :].T, axis=0, keepdims=True)


def first_pass(frame, targets, rows, weights, scales, scores, sums, part, limits):
    part[...] = jnp.zeros_like(part)
    limits[...] = jnp.where(frame[COLUMNS_AT : COLUMNS_AT + COLUMN_BLOCKS, :] > 0.0, 0.0, ABSENT)
    scale = scales[0:1, :]
    twice = 2.0 * scale

    @pl.loop(0, COLUMN_BLOCKS // 2, unroll=8)
    def _(pair):
        first = pair * 2
        block = targets[pl.ds(first, 2)].reshape(2 * CELLS, WIDTH)
        products = lax.dot_general(
            rows[...], block, (((1,), (1,)), ((), ())), preferred_element_type=F32
        )
        running = part[...]
        for half in range(2):
            wide = targets[first + half].astype(F32)
            squares = wide * wide
            norms = jnp.sum((squares[:, :CELLS] + squares[:, CELLS:]).T, axis=0, keepdims=True)
            tile = (weights[...] + norms * scale) - twice * products[
                :, half * CELLS : (half + 1) * CELLS
            ]
            scores[first + half] = tile
            running = running + jnp.exp2(limits[pl.ds(first + half, 1), :] - tile)
        part[...] = running

    for k in range(ROW_BLOCKS):
        sums[k : k + 1, :] = lane_sums(part, k)
    sums[4:5, :] = frame[GROWTH : GROWTH + 1, :]
    sums[5:8, :] = jnp.zeros((3, CELLS), F32)


def column_pass(frame, alpha, scores, out, spread_out, gathered):
    for k in range(ROW_BLOCKS):
        present = frame[ROWS_AT + k : ROWS_AT + k + 1, :] > 0.0
        limit = jnp.where(present, alpha[k] * LOG2E, ABSENT)
        spread_out[k * CELLS : (k + 1) * CELLS, :] = jnp.broadcast_to(limit, (CELLS, CELLS)).T

    def strip(number, running):
        at = pl.ds(pl.multiple_of(number * STRIP, STRIP), STRIP)
        limit = spread_out[at, :]
        more = []
        for i, total in enumerate(running):
            terms = jnp.exp2(limit - scores[i, at, :])
            more.append(total + jnp.sum(terms.reshape(STRIP // 8, 8, CELLS), axis=0))
        return tuple(more)

    zeros = (jnp.zeros((8, CELLS), F32),) * COLUMN_BLOCKS
    for i, total in enumerate(lax.fori_loop(0, ROWS // STRIP, strip, zeros, unroll=8)):
        gathered[i : i + 1, :] = jnp.sum(total, axis=0, keepdims=True)
    out[...] = jnp.broadcast_to(gathered[...][None], out.shape)


def new_alphas(frame, parts, log_p):
    alphas = []
    for k in range(ROW_BLOCKS):
        total = parts[0][k : k + 1, :]
        for j in range(1, ROW_BLOCKS):
            total = total + parts[j][(k ^ j) : (k ^ j) + 1, :]
        present = frame[ROWS_AT + k : ROWS_AT + k + 1, :] > 0.0
        alphas.append(jnp.where(present, TAU * (log_p[k] - jnp.log(total)), 0.0))
    return alphas


def first_columns(frame, p0, p1, p2, p3, scores, log_out, out, spread_out, gathered):
    n_s = frame[N_S : N_S + 1, :]
    parts = (p0, p1, p2, p3)
    log_p = [jnp.log(part[4:5, :] / n_s) for part in parts]
    for k in range(ROW_BLOCKS):
        log_out[k : k + 1, :] = log_p[k]
    column_pass(frame, new_alphas(frame, parts, log_p), scores, out, spread_out, gathered)


def last_columns(
    frame, log_p, p0, p1, p2, p3, scores, weights, alpha_out, out, spread_out, gathered
):
    n_s = frame[N_S : N_S + 1, :]
    log_rows = [log_p[k : k + 1, :] for k in range(ROW_BLOCKS)]
    alphas = new_alphas(frame, (p0, p1, p2, p3), log_rows)
    alpha_out[...] = alphas[0]
    for k in range(ROW_BLOCKS):
        present = frame[ROWS_AT + k : ROWS_AT + k + 1, :]
        weights[k : k + 1, :] = present * n_s * jnp.exp(alphas[k])
    column_pass(frame, alphas, scores, out, spread_out, gathered)


def row_pass(frame, parts, scores, part, limits):
    n_t = frame[N_T : N_T + 1, :]
    total = jnp.sum(parts[...], axis=0)
    beta = TAU * (-jnp.log(n_t) - jnp.log(total))
    present = frame[COLUMNS_AT : COLUMNS_AT + COLUMN_BLOCKS, :] > 0.0
    limits[...] = jnp.where(present, beta * LOG2E, ABSENT)

    @pl.loop(0, ROWS // STRIP, unroll=8)
    def _(number):
        at = pl.ds(pl.multiple_of(number * STRIP, STRIP), STRIP)
        running = jnp.exp2(limits[0:1, :] - scores[0, at, :])
        for i in range(1, COLUMN_BLOCKS):
            running = running + jnp.exp2(limits[i : i + 1, :] - scores[i, at, :])
        part[at, :] = running

    return jnp.where(present, beta, 0.0)


def second_rows(frame, parts, scores, sums, part, limits):
    row_pass(frame, parts, scores, part, limits)
    for k in range(ROW_BLOCKS):
        sums[k : k + 1, :] = lane_sums(part, k)


def last_rows(frame, parts, scores, weights, beta_out, q0, q1, q2, q3, part, limits, betas):
    betas[...] = row_pass(frame, parts, scores, part, limits)
    place = lax.axis_index("x") * 4 + lax.axis_index("y")
    beta_out[...] = betas[pl.ds(place, 1), :]
    for k, out in enumerate((q0, q1, q2, q3)):
        present = frame[ROWS_AT + k : ROWS_AT + k + 1, :] > 0.0
        out[...] = jnp.where(present, weights[k : k + 1, :] * lane_sums(part, k), 0.0)


def outputs(alpha, beta, q0, q1, q2, q3, alpha_out, beta_out, mass_out):
    alpha_out[...] = alpha[...]
    beta_out[...] = beta[...]
    mass_out[...] = (q0[...] + q1[...]) + (q2[...] + q3[...])


def in_hbm(array):
    return pltpu.with_memory_space_constraint(array, pltpu.HBM)


def swapped(value, axis):
    return lax.ppermute(value, axis, [(0, 1), (1, 0)])


def across(value, k):
    return lax.ppermute(value, ROW_AXES, [(d, d ^ k) for d in range(4)])


def back(value, k):
    moves = [(z * 4 + g, (z ^ k) * 4 + g - 1) for z in range(2) for g in range(1, 4)]
    return lax.ppermute(value, ("z", "g"), moves)


def exchanged(copies):
    return lax.all_to_all(copies, COLUMN_AXES, split_axis=0, concat_axis=0, tiled=True)


def local(features, last_features, growth, cell_counts):
    part = pltpu.VMEM((ROWS, CELLS), F32)
    limits = pltpu.VMEM((COLUMN_BLOCKS, CELLS), F32)
    some_cells = shape(CELLS, WIDTH, dtype=BF16)
    row_parts = shape(8, CELLS)
    column_parts = shape(COLUMN_BLOCKS, COLUMN_BLOCKS, CELLS)

    with jax.named_scope("moments"):
        copies, own, last, frame = call(
            local_sums,
            (shape(COLUMN_BLOCKS, 8, CELLS), some_cells, some_cells, shape(FRAME, CELLS)),
            4,
            (
                pltpu.VMEM((1, CELLS, WIDTH), BF16),
                pltpu.VMEM((CELLS, WIDTH), BF16),
                pltpu.VMEM((1, CELLS), F32),
                pltpu.SMEM((5,), jnp.int32),
                pltpu.SemaphoreType.DMA((4,)),
            ),
            space=pltpu.HBM,
            name="local_sums",
        )(*(in_hbm(a) for a in (features, last_features, growth, cell_counts)))
        messages = exchanged(copies)
    with jax.named_scope("gather"):
        targets = call(parcel, shape(COLUMN_BLOCKS, CELLS, WIDTH, dtype=BF16), 3, name="parcel")(
            frame, back(features[0], 0), last
        )
        anywhere = pl.BlockSpec(memory_space=pl.ANY)
        vmem = pl.BlockSpec(memory_space=pltpu.VMEM)
        sums, own, targets = pl.pallas_call(
            group_sums,
            out_shape=(
                row_parts,
                some_cells,
                shape(COLUMN_BLOCKS, CELLS, WIDTH, dtype=BF16),
            ),
            in_specs=[vmem] * 2 + [anywhere],
            out_specs=(vmem, vmem, anywhere),
            input_output_aliases={2: 2},
            compiler_params=pltpu.CompilerParams(vmem_limit_bytes=16 * 1024 * 1024),
            name="group_sums",
        )(messages, own, targets)
        targets = exchanged(targets)
        sums, near = call(
            core_sums, (row_parts, shape(2 * CELLS, WIDTH, dtype=BF16)), 4, name="core_sums"
        )(sums, swapped(sums, "c"), own, swapped(own, "c"))
        sums = (sums, swapped(sums, "z"), back(sums, 0), back(sums, 1))
        ready = call(
            prepared,
            (shape(ROWS, WIDTH, dtype=BF16), shape(ROWS, CELLS), row_parts),
            7,
            name="prepared",
        )(frame, *sums, near, swapped(near, "z"))

    def row_exchange(sums):
        return [sums] + [across(sums, k) for k in range(1, ROW_BLOCKS)]

    with jax.named_scope("first_rows"):
        scores, sums = call(
            first_pass,
            (shape(COLUMN_BLOCKS, ROWS, CELLS), row_parts),
            5,
            (part, limits),
            name="first_pass",
        )(frame, targets, *ready)
    with jax.named_scope("first_columns"):
        log_p, copies = call(
            first_columns,
            (shape(ROW_BLOCKS, CELLS), column_parts),
            6,
            (part, limits),
            name="first_columns",
        )(frame, *row_exchange(sums), scores)
        parts = exchanged(copies)
    with jax.named_scope("second_rows"):
        sums = call(second_rows, shape(ROW_BLOCKS, CELLS), 3, (part, limits), name="second_rows")(
            frame, parts, scores
        )
    with jax.named_scope("last_columns"):
        weights, source_pot, copies = call(
            last_columns,
            (shape(ROW_BLOCKS, CELLS), shape(1, CELLS), column_parts),
            7,
            (part, limits),
            name="last_columns",
        )(frame, log_p, *row_exchange(sums), scores)
        parts = exchanged(copies)
    with jax.named_scope("mass"):
        target_pot, *masses = call(
            last_rows, (shape(1, CELLS),) * 5, 4, (part, limits, limits), name="last_rows"
        )(frame, parts, scores, weights)
        masses = [masses[0]] + [across(masses[k], k) for k in range(1, ROW_BLOCKS)]
        return call(outputs, (shape(1, CELLS),) * 3, 6, name="outputs")(
            source_pot, target_pot, *masses
        )


def solution(mesh):
    fine = Mesh(mesh.devices.reshape(SIZES), AXES)
    blk = ("x", "z", "y", "c")
    return jax.shard_map(
        local,
        mesh=fine,
        in_specs=(P("g", blk, None), P(blk, None), P("g", blk), P()),
        out_specs=(P("g", blk),) * 3,
        check_vma=False,
    )
```
